32 devices in a mesh: dom: 4 (over z), ml: 8 (over y, x, core).
Axes of the slice: x: 2, y: 2, z: 4, core: 2. Of those that a mesh axis runs over, the one named last changes fastest.
Arguments:
- mm_positions: float32 [3, 65536], P(None, ('dom', 'ml')), may hold values from -6 to 6
- mm_charge: float32 [65536], P(('dom', 'ml')), may hold values from -1 to 1
- mm_tiles: int32 [512, 8], P(('dom', 'ml')), may hold values from 0 to 47, as said below
- ml_feat: bfloat16 [32, 512, 128], P('dom', 'ml'), may hold values from -6 to 6
- ml_positions: float32 [32, 3, 512], P('dom', None, 'ml'), may hold values from -6 to 6
- ml_neighbours: int32 [32, 32, 512], P('dom', None, 'ml'), may hold values from 0 to 511
- msg_weight: bfloat16 [2, 128, 128], replicated, may hold values from -0.5 to 0.5
- radial_weight: float32 [2, 8, 128], replicated, may hold values from -5 to 5
- out_weight: bfloat16 [2, 128, 128], replicated, may hold values from -0.5 to 0.5
- read_weight: bfloat16 [128, 256], replicated, may hold values from -0.5 to 0.5
Outputs:
- mm_force: float32 [3, 65536], P(None, ('dom', 'ml'))
- ml_force: float32 [32, 3, 512], P('dom', None, 'ml')
The draws below stay inside these ranges and needn't reach their ends.
Inputs may be any that keep to these rules, and one draw needn't show every extreme that they name: `mm_tiles`: for each tile of a device, 8 distinct positions among the 16 tiles of the previous device along dom+ml (wrapping), its own tiles and the next device's, in that order; at least one lies among the previous device's tiles and at least one among the next device's. `ml_neighbours`: indices of atoms within the same patch.
All inputs are finite; a program needn't handle non-finite values.
Results may differ from the reference program's by a relative error of at most 0.007.
Values may be sent and summed in bfloat16 or wider, within the bound.
A program may use at most 320 MiB of HBM per device.

```python
import math
import jax
import jax.numpy as jnp
from jax import lax

F = 128
LAYERS = 2
NB = 8
K = 32
P_SIZE = 512
TILE = 128
TILES_DEV = 16
NEIGHBOR_TILES = 8
NP = 32
NTILE = 512
NMM = 65536


def draw_mm_tiles(key, part):
    key = jax.random.fold_in(key, 11)
    window = 3 * TILES_DEV
    score_key, low_key, high_key = jax.random.split(key, 3)
    ranking_values = jax.random.randint(score_key, (NTILE, window), 0, 1 << 20)
    ranking_values = ranking_values * window + jnp.arange(window, dtype=jnp.int32)[None, :]
    lower_selection = jax.random.randint(low_key, (NTILE, 1), 0, TILES_DEV)
    upper_selection = jax.random.randint(high_key, (NTILE, 1), 2 * TILES_DEV, 3 * TILES_DEV)
    column_slots = jnp.arange(window, dtype=jnp.int32)[None, :]
    extra_reward = jnp.where(column_slots == lower_selection, 1 << 28, 0) + jnp.where(column_slots == upper_selection, 1 << 28, 0)
    selected_entries = lax.top_k(ranking_values + extra_reward, NEIGHBOR_TILES)[1]
    return selected_entries.astype(jnp.int32)


def place_ends(values, own_key, least, high):
    index_at = [jax.random.randint(jax.random.fold_in(own_key, axis), (), 0, length) for axis, length in enumerate(values.shape)]
    longest = values.shape.index(max(values.shape))
    beside = index_at[:longest] + [(index_at[longest] + 1) % values.shape[longest]] + index_at[longest + 1:]
    return values.at[tuple(index_at)].set(least).at[tuple(beside)].set(high)


def level_of(own_key, dims, cuts, least, largest):
    factor_of = 1.0
    for position, parts in cuts:
        draws = jax.random.uniform(jax.random.fold_in(jax.random.fold_in(own_key, 6), position), (parts,), jnp.float32, least / len(cuts), largest / len(cuts))
        factor_of = factor_of * jnp.repeat(jnp.exp(draws), dims[position] // parts).reshape((-1,) + (1,) * (len(dims) - 1 - position))
    return factor_of


def scatter_about(rng, shape, spread, most, cuts=(), kind=jnp.bfloat16):
    values = jax.random.normal(rng, shape, jnp.float32) * spread
    if len(cuts) > 0:
        values = level_of(rng, shape, cuts, -0.22, 0.18) * values
    return jnp.clip(values, min=-most, max=most).astype(kind)


def setup_inputs(seed: int = 0) -> dict:
    arg_keys = jax.random.split(jax.random.key(seed), 11)
    mm_positions = scatter_about(arg_keys[0], (3, NMM), 1.0, 6.0, ((1, 32),), jnp.float32)
    mm_charge = jnp.clip(jax.random.uniform(arg_keys[1], (NMM,), jnp.float32, -1.0, 1.0) * level_of(arg_keys[1], (NMM,), ((0, 32),), -0.4, 0.0), -1.0, 1.0)
    mm_tiles = draw_mm_tiles(jax.random.fold_in(arg_keys[10], 71), 0)
    ml_feat = scatter_about(arg_keys[3], (NP, P_SIZE, F), 1.0, 6.0, ((0, 4), (1, 8)))
    ml_positions = scatter_about(arg_keys[4], (NP, 3, P_SIZE), 1.5, 6.0, ((0, 4), (2, 8)), jnp.float32)
    ml_neighbours = place_ends(jax.random.randint(arg_keys[5], (NP, K, P_SIZE), 0, P_SIZE), jax.random.fold_in(arg_keys[5], 1), 0, P_SIZE - 1).astype(jnp.int32)
    msg_weight = scatter_about(arg_keys[6], (LAYERS, F, F), F ** -0.5, 0.5)
    radial_weight = scatter_about(arg_keys[7], (LAYERS, NB, F), 1.0, 5.0, (), jnp.float32)
    out_weight = scatter_about(arg_keys[8], (LAYERS, F, F), F ** -0.5, 0.5)
    read_weight = scatter_about(arg_keys[9], (F, 2 * F), F ** -0.5, 0.5)
    return dict(mm_positions=mm_positions, mm_charge=mm_charge, mm_tiles=mm_tiles, ml_feat=ml_feat, ml_positions=ml_positions, ml_neighbours=ml_neighbours, msg_weight=msg_weight, radial_weight=radial_weight, out_weight=out_weight, read_weight=read_weight)


RADIUS = 6.0
SOFTEN = 1.0
COULOMB = 0.5

def pair_force(own_tile, near_tiles):
    offsets = own_tile[:3, None, :, None] - near_tiles[:3, :, None, :]
    squared = lax.optimization_barrier(jnp.sum(offsets * offsets, axis=0)) + SOFTEN
    inverse = 1.0 / (squared * jnp.sqrt(squared))
    strength = COULOMB * own_tile[3][None, :, None] * near_tiles[3][:, None, :] * inverse
    return lax.optimization_barrier(jnp.sum(strength[None] * offsets, axis=(1, 3)))

def patch_model(pieces, msg_weight, radial_weight, out_weight, read_weight):
    features, positions, neighbours = pieces
    offsets = positions[:, neighbours] - positions[:, None, :]
    distance = jnp.sqrt(lax.optimization_barrier(jnp.sum(offsets * offsets, axis=0)) + 1.0)
    envelope = 0.5 * (jnp.cos(jnp.pi * jnp.minimum(distance / RADIUS, 1.0)) + 1.0)
    centers = jnp.arange(NB).astype(jnp.float32) * (RADIUS / NB)
    radial_basis = jnp.exp(-2.0 * (distance[None] - centers[:, None, None]) ** 2) * envelope[None]
    norm_factor = 1.0 / math.sqrt(K)
    hidden = features
    for layer_index in range(LAYERS):
        mixed_feat = jnp.dot(hidden, msg_weight[layer_index], preferred_element_type=jnp.float32).astype(jnp.bfloat16)
        radial = jnp.einsum('nkp,nc->kpc', radial_basis, radial_weight[layer_index].astype(jnp.float32), precision=lax.Precision.HIGHEST)
        message = lax.optimization_barrier(jnp.sum(radial * mixed_feat[neighbours].astype(jnp.float32), axis=0)) * norm_factor
        active = jax.nn.silu(message).astype(jnp.bfloat16)
        update = jnp.dot(active, out_weight[layer_index], preferred_element_type=jnp.float32)
        hidden = (hidden.astype(jnp.float32) + update).astype(jnp.bfloat16)
    readout = jnp.dot(hidden, read_weight, preferred_element_type=jnp.float32).astype(jnp.bfloat16)
    query_feat = readout[:, :F].astype(jnp.float32)
    key_feat = readout[:, F:].astype(jnp.float32)
    strength = jnp.einsum('pc,kpc->kp', query_feat, key_feat[neighbours]) / F * envelope
    return lax.optimization_barrier(jnp.sum(strength[None] * offsets, axis=1))

def reference(mm_positions, mm_charge, mm_tiles, ml_feat, ml_positions, ml_neighbours, msg_weight, radial_weight, out_weight, read_weight):
    mm_atoms = jnp.concatenate([mm_positions, mm_charge[None]], axis=0).reshape(4, NTILE, TILE)

    def tile_force(tile_index):
        slab_index = tile_index // TILES_DEV
        global_tile = (slab_index * TILES_DEV - TILES_DEV + mm_tiles[tile_index]) % NTILE
        return pair_force(mm_atoms[:, tile_index], mm_atoms[:, global_tile])
    tile_forces = lax.map(tile_force, jnp.arange(NTILE).astype(jnp.int32))
    mm_force = tile_forces.transpose(1, 0, 2).reshape(3, NMM)

    def run_patch(pieces):
        return patch_model(pieces, msg_weight, radial_weight, out_weight, read_weight)
    ml_force = lax.map(run_patch, (ml_feat, ml_positions, ml_neighbours))
    return (mm_force, ml_force)
```

```python
import functools
import math

import jax
import jax.numpy as jnp
from jax import lax
from jax.experimental import pallas as pl
from jax.experimental.pallas import tpu as pltpu
from jax.sharding import PartitionSpec as P

TILE = 128
RADIUS = 6.0
SOFTEN = 1.0
COULOMB = 0.5
F32 = jnp.float32
BF16 = jnp.bfloat16
MESH = pl.DeviceIdType.MESH
ANY = pl.BlockSpec(memory_space=pl.ANY)
VMEM = pl.BlockSpec(memory_space=pltpu.VMEM)


def split3(x):
    high = x.astype(BF16).astype(F32)
    rest = x - high
    middle = rest.astype(BF16).astype(F32)
    return high, middle, (rest - middle).astype(BF16).astype(F32)


def last_row(shape):
    return lax.broadcasted_iota(jnp.int32, shape, 0) == 3


def left_factor(xyz):
    norm = jnp.sum(xyz * xyz, axis=0, keepdims=True)
    high, middle, low = split3(jnp.concatenate([xyz, norm], axis=0))
    last = last_row(high.shape)
    one = jnp.ones_like(high)
    groups = [
        high,
        jnp.where(last, middle, high),
        jnp.where(last, low, middle),
        jnp.where(last, one, high),
        jnp.where(last, one, low),
        jnp.where(last, one, middle),
        jnp.zeros_like(high),
        jnp.zeros_like(high),
    ]
    return jnp.concatenate(groups, axis=0)


def right_factor(xyz):
    norm = jnp.sum(xyz * xyz, axis=0, keepdims=True) + SOFTEN
    high, middle, low = split3(jnp.concatenate([-2.0 * xyz, norm], axis=0))
    last = last_row(high.shape)
    one = jnp.ones_like(high)
    groups = [
        jnp.where(last, one, high),
        jnp.where(last, one, middle),
        jnp.where(last, one, high),
        low,
        high,
        middle,
        jnp.zeros_like(high),
        jnp.zeros_like(high),
    ]
    return jnp.concatenate(groups, axis=0).astype(BF16)


def moment_rows(xyz, weight):
    rows = jnp.concatenate([xyz * weight, weight], axis=0)
    high, middle, low = split3(rows)
    return jnp.concatenate([high, middle, low, jnp.zeros_like(high)], axis=0).astype(BF16)


def folded(moments):
    return moments[0:4] + moments[4:8] + moments[8:12]


def dot(a, b):
    return jnp.dot(a, b, preferred_element_type=F32)


def half_wave(u):
    x = u * (math.pi / 2)
    y = x * x
    p = -1.0 / 39916800
    for c in (1.0 / 362880, -1.0 / 5040, 1.0 / 120, -1.0 / 6, 1.0):
        p = p * y + c
    return p * x


def kernel(
    shape,
    mm_pos,
    mm_charge,
    mm_tiles,
    feat,
    pos,
    nbr,
    msg_w,
    rad_w,
    out_w,
    read_w,
    mm_out,
    ml_out,
    win_p,
    win_q,
    tiles,
    feat_buf,
    pos_buf,
    nbr_buf,
    msg_v,
    rad_v,
    out_v,
    read_v,
    near_v,
    near_r,
    own_u,
    word_s,
    value_s,
    basis,
    weight_s,
    rad_cols,
    stage,
    force_buf,
    local_sem,
    halo_send,
    halo_recv,
    ml_send,
    ml_recv,
    back_send,
    back_recv,
):
    doms, mls = shape
    patches = feat.shape[0]
    atoms = feat.shape[1]
    nbrs = nbr.shape[1]
    psize = mls * atoms
    layers, nb, width = rad_w.shape
    tile_nbrs, tile_count = mm_tiles.shape

    dom = lax.axis_index("dom")
    me = lax.axis_index("ml")
    flat = dom * mls + me
    after = lax.rem(flat + 1, doms * mls)
    before = lax.rem(flat + doms * mls - 1, doms * mls)
    sides = [(before // mls, lax.rem(before, mls)), (after // mls, lax.rem(after, mls))]
    my_patch = lax.rem(me, patches)

    local = [
        pltpu.make_async_copy(mm_pos, win_p.at[1], local_sem.at[0]),
        pltpu.make_async_copy(mm_charge, win_q.at[1], local_sem.at[1]),
        pltpu.make_async_copy(mm_tiles, tiles, local_sem.at[2]),
        pltpu.make_async_copy(msg_w, msg_v, local_sem.at[3]),
        pltpu.make_async_copy(rad_w, rad_v, local_sem.at[4]),
        pltpu.make_async_copy(out_w, out_v, local_sem.at[5]),
        pltpu.make_async_copy(read_w, read_v, local_sem.at[6]),
        pltpu.make_async_copy(nbr.at[my_patch], nbr_buf.at[me], local_sem.at[7]),
        pltpu.make_async_copy(pos, pos_buf.at[me], local_sem.at[8]),
        pltpu.make_async_copy(feat.at[my_patch], feat_buf.at[me], local_sem.at[9]),
    ]
    for copy in local:
        copy.start()

    barrier = pltpu.get_barrier_semaphore()
    for side in sides:
        pl.semaphore_signal(barrier, inc=1, device_id=side, device_id_type=MESH)
    peers = [lax.rem(me + o, mls) for o in range(1, mls)]
    for peer in peers:
        pl.semaphore_signal(barrier, inc=1, device_id=(dom, peer), device_id_type=MESH)
    pl.semaphore_wait(barrier, mls + 1)

    halo = []
    for k, (side, slab) in enumerate(zip(sides, (2, 0))):
        for m, (src, dst) in enumerate(((mm_pos, win_p), (mm_charge, win_q))):
            halo.append(
                pltpu.make_async_remote_copy(
                    src_ref=src,
                    dst_ref=dst.at[slab],
                    send_sem=halo_send.at[2 * k + m],
                    recv_sem=halo_recv.at[2 * k + m],
                    device_id=side,
                    device_id_type=MESH,
                )
            )
    for copy in halo:
        copy.start()
    moves = []
    for m, (src, dst) in enumerate(((nbr, nbr_buf), (pos, pos_buf), (feat, feat_buf))):
        group = []
        for o, peer in enumerate(peers):
            group.append(
                pltpu.make_async_remote_copy(
                    src_ref=src if m == 1 else src.at[lax.rem(peer, patches)],
                    dst_ref=dst.at[me],
                    send_sem=ml_send.at[m, o],
                    recv_sem=ml_recv.at[m, o],
                    device_id=(dom, peer),
                    device_id_type=MESH,
                )
            )
        for copy in group:
            copy.start()
        moves.append(group)

    for copy in local:
        copy.wait()
    center = nb // 2
    step = RADIUS / nb
    factors = [
        math.exp(-2.0 * (step * (n - center)) ** 2) / math.sqrt(nbrs) for n in range(nb)
    ]
    for l in range(layers):
        columns = jnp.concatenate([rad_v[l], jnp.zeros((width - nb, width), F32)], axis=0).T
        for n in range(nb):
            rad_cols[l, n] = jnp.broadcast_to(columns[:, n : n + 1] * factors[n], (width, TILE))
    left = left_factor(win_p[1])
    for t in range(tile_count):
        own_u[t] = left[:, t * TILE : (t + 1) * TILE].T.astype(BF16)

    def near_slab(slab):
        xyz = win_p[slab]
        right = right_factor(xyz)
        rows = moment_rows(xyz, win_q[slab])
        for t in range(tile_count):
            near_v[slab * tile_count + t] = right[:, t * TILE : (t + 1) * TILE]
            near_r[slab * tile_count + t] = rows[:, t * TILE : (t + 1) * TILE]

    near_slab(1)
    for copy in halo:
        copy.wait_recv()
    near_slab(0)
    near_slab(2)

    def mm_tile(t, carry):
        own = own_u[t]
        total = jnp.zeros((16, TILE), F32)
        for c in range(0, tile_nbrs, 2):
            one, two = tiles[c, t], tiles[c + 1, t]
            right = jnp.concatenate([near_v[one], near_v[two]], axis=1)
            rows = jnp.concatenate([near_r[one], near_r[two]], axis=1)
            inverse = lax.rsqrt(dot(own, right))
            cubed = (inverse * inverse * inverse).astype(BF16)
            total = total + lax.dot_general(
                rows, cubed, (((1,), (1,)), ((), ())), preferred_element_type=F32
            )
        at = pl.ds(pl.multiple_of(t * TILE, TILE), TILE)
        sums = folded(total)
        force = win_p[1, :, at] * sums[3:4] - sums[0:3]
        mm_out[:, at] = force * (COULOMB * win_q[1, :, at])
        return carry

    first_half = tile_count // 2
    lax.fori_loop(0, first_half, mm_tile, 0)

    for copy in moves[0] + moves[1]:
        copy.wait_recv()
    listed = jnp.concatenate([nbr_buf[d] for d in range(mls)], axis=1)
    words = psize // 4
    word_s[...] = lax.rem(listed, words)
    value_s[...] = jnp.left_shift(1, 8 * (listed // words))
    xyz = jnp.concatenate([pos_buf[d, :, my_patch, :] for d in range(mls)], axis=1)
    senders = left_factor(xyz).T.astype(BF16)
    receivers = right_factor(xyz)
    rows = moment_rows(xyz, jnp.ones_like(xyz[0:1]))
    for ib in range(psize // TILE):
        at = slice(ib * TILE, (ib + 1) * TILE)
        place = lax.broadcasted_iota(jnp.int32, (words, TILE), 0)
        counts = jnp.zeros((words, TILE), jnp.int32)
        for k in range(nbrs):
            hit = place == word_s[k : k + 1, at]
            counts = counts + jnp.where(hit, value_s[k : k + 1, at], 0)
        for b in range(4):
            rows_at = slice(b * words, (b + 1) * words)
            count = (jnp.right_shift(counts, 8 * b) & 255).astype(F32)
            squared = dot(senders[rows_at], receivers[:, at])
            distance = jnp.minimum(squared * lax.rsqrt(squared), RADIUS)
            wave = half_wave(1.0 - distance * (1.0 / RADIUS))
            weight = count * (wave * wave)
            weight_s[rows_at, at] = weight
            shifted = distance - center * step
            middle = weight * jnp.exp(-2.0 * shifted * shifted)
            basis[center, rows_at, at] = middle.astype(BF16)
            up = jnp.exp(4.0 * step * shifted)
            value = middle
            for n in range(center + 1, nb):
                value = value * up
                basis[n, rows_at, at] = value.astype(BF16)
            down = jnp.exp(-4.0 * step * shifted)
            value = middle
            for n in range(center - 1, -1, -1):
                value = value * down
                basis[n, rows_at, at] = value.astype(BF16)

    for copy in moves[2]:
        copy.wait_recv()
    hidden = feat_buf[...].reshape(psize, width).astype(F32).T.astype(BF16)
    for l in range(layers):
        mixed = dot(msg_v[l].astype(F32).T.astype(BF16), hidden).astype(BF16)
        message = jnp.zeros((width, psize), F32)
        for n in range(nb):
            column = jnp.concatenate([rad_cols[l, n]] * (psize // TILE), axis=1)
            message = message + column * dot(mixed, basis[n])
        active = (message / (1.0 + jnp.exp(-message))).astype(BF16)
        update = dot(out_v[l].astype(F32).T.astype(BF16), active)
        hidden = (hidden.astype(F32) + update).astype(BF16)
    readout = dot(read_v[...].astype(F32).T.astype(BF16), hidden)
    query = readout[:width].astype(BF16)
    key = readout[width:].T.astype(BF16)
    strength = dot(key, query) * weight_s[...] * (1.0 / width)
    strong = strength.astype(BF16)
    weak = (strength - strong.astype(F32)).astype(BF16)
    sums = folded(dot(rows, strong) + dot(rows, weak))
    force = sums[0:3] - xyz * sums[3:4]
    for d in range(mls):
        stage[d] = force[:, d * atoms : (d + 1) * atoms]
    group = me - my_patch
    returns = []
    for o in range(1, patches):
        owner = group + lax.rem(my_patch + o, patches)
        copy = pltpu.make_async_remote_copy(
            src_ref=stage.at[owner],
            dst_ref=force_buf.at[my_patch],
            send_sem=back_send.at[o - 1],
            recv_sem=back_recv.at[o - 1],
            device_id=(dom, owner),
            device_id_type=MESH,
        )
        copy.start()
        returns.append(copy)
    own = pltpu.make_async_copy(stage.at[me], force_buf.at[my_patch], local_sem.at[0])
    own.start()

    lax.fori_loop(first_half, tile_count, mm_tile, 0)

    for copy in halo:
        copy.wait_send()
    for group in moves:
        for copy in group:
            copy.wait_send()
    own.wait()
    for copy in returns:
        copy.wait()
    for p in range(patches):
        ml_out[:, p, :] = force_buf[p]


def on_device(
    shape,
    mm_positions,
    mm_charge,
    mm_tiles,
    ml_feat,
    ml_positions,
    ml_neighbours,
    msg_weight,
    radial_weight,
    out_weight,
    read_weight,
):
    mls = shape[1]
    patches, atoms, width = ml_feat.shape
    nbrs = ml_neighbours.shape[1]
    psize = mls * atoms
    layers, nb, _ = radial_weight.shape
    count = mm_positions.shape[1]
    tile_count = count // TILE
    dma = pltpu.SemaphoreType.DMA
    mm_force, ml_force = pl.pallas_call(
        functools.partial(kernel, shape),
        out_shape=(
            jax.ShapeDtypeStruct((3, count), F32),
            jax.ShapeDtypeStruct((3, patches, atoms), F32),
        ),
        in_specs=[ANY] * 10,
        out_specs=(VMEM, VMEM),
        scratch_shapes=[
            pltpu.VMEM((3, 3, count), F32),
            pltpu.VMEM((3, 1, count), F32),
            pltpu.SMEM(mm_tiles.shape[::-1], jnp.int32),
            pltpu.VMEM((mls, atoms, width), BF16),
            pltpu.VMEM((mls, 3, patches, atoms), F32),
            pltpu.VMEM((mls, nbrs, atoms), jnp.int32),
            pltpu.VMEM(msg_weight.shape, BF16),
            pltpu.VMEM(radial_weight.shape, F32),
            pltpu.VMEM(out_weight.shape, BF16),
            pltpu.VMEM(read_weight.shape, BF16),
            pltpu.VMEM((3 * tile_count, 32, TILE), BF16),
            pltpu.VMEM((3 * tile_count, 16, TILE), BF16),
            pltpu.VMEM((tile_count, TILE, 32), BF16),
            pltpu.VMEM((nbrs, psize), jnp.int32),
            pltpu.VMEM((nbrs, psize), jnp.int32),
            pltpu.VMEM((nb, psize, psize), BF16),
            pltpu.VMEM((psize, psize), F32),
            pltpu.VMEM((layers, nb, width, TILE), F32),
            pltpu.VMEM((mls, 3, atoms), F32),
            pltpu.VMEM((patches, 3, atoms), F32),
            dma((10,)),
            dma((4,)),
            dma((4,)),
            dma((3, mls)),
            dma((3, mls)),
            dma((patches,)),
            dma((patches,)),
        ],
        compiler_params=pltpu.CompilerParams(
            collective_id=0, has_side_effects=True, vmem_limit_bytes=60 * 1024 * 1024
        ),
        name="force_step",
    )(
        mm_positions,
        mm_charge.reshape(1, count),
        mm_tiles.T,
        ml_feat,
        ml_positions.transpose(1, 0, 2),
        ml_neighbours,
        msg_weight,
        radial_weight,
        out_weight,
        read_weight,
    )
    return mm_force, ml_force.transpose(1, 0, 2)


def solution(mesh):
    shape = (mesh.shape["dom"], mesh.shape["ml"])
    in_specs = (
        P(None, ("dom", "ml")),
        P(("dom", "ml")),
        P(("dom", "ml"), None),
        P("dom", "ml", None),
        P("dom", None, "ml"),
        P("dom", None, "ml"),
        P(),
        P(),
        P(),
        P(),
    )
    out_specs = (P(None, ("dom", "ml")), P("dom", None, "ml"))
    return jax.shard_map(
        functools.partial(on_device, shape),
        mesh=mesh,
        in_specs=in_specs,
        out_specs=out_specs,
        check_vma=False,
    )
```

```python
import functools
import math

import jax
import jax.numpy as jnp
from jax import lax
from jax.experimental import pallas as pl
from jax.experimental.pallas import tpu as pltpu
from jax.sharding import PartitionSpec as P

TILE = 128
RADIUS = 6.0
SOFTEN = 1.0
COULOMB = 0.5
CHUNK = 32
F32 = jnp.float32
BF16 = jnp.bfloat16
MESH = pl.DeviceIdType.MESH
ANY = pl.BlockSpec(memory_space=pl.ANY)
VMEM = pl.BlockSpec(memory_space=pltpu.VMEM)


def split3(x):
    high = x.astype(BF16).astype(F32)
    rest = x - high
    middle = rest.astype(BF16).astype(F32)
    return high, middle, (rest - middle).astype(BF16).astype(F32)


def last_row(shape):
    return lax.broadcasted_iota(jnp.int32, shape, 0) == 3


def left_factor(xyz):
    norm = jnp.sum(xyz * xyz, axis=0, keepdims=True)
    high, middle, low = split3(jnp.concatenate([xyz, norm], axis=0))
    last = last_row(high.shape)
    one = jnp.ones_like(high)
    groups = [
        high,
        jnp.where(last, middle, high),
        jnp.where(last, low, middle),
        jnp.where(last, one, high),
        jnp.where(last, one, low),
        jnp.where(last, one, middle),
        jnp.zeros_like(high),
        jnp.zeros_like(high),
    ]
    return jnp.concatenate(groups, axis=0)


def right_factor(xyz):
    norm = jnp.sum(xyz * xyz, axis=0, keepdims=True) + SOFTEN
    high, middle, low = split3(jnp.concatenate([-2.0 * xyz, norm], axis=0))
    last = last_row(high.shape)
    one = jnp.ones_like(high)
    groups = [
        jnp.where(last, one, high),
        jnp.where(last, one, middle),
        jnp.where(last, one, high),
        low,
        high,
        middle,
        jnp.zeros_like(high),
        jnp.zeros_like(high),
    ]
    return jnp.concatenate(groups, axis=0).astype(BF16)


def moment_rows(xyz, weight):
    rows = jnp.concatenate([xyz * weight, weight], axis=0)
    high, middle, low = split3(rows)
    return jnp.concatenate([high, middle, low, jnp.zeros_like(high)], axis=0).astype(BF16)


def folded(moments):
    return moments[0:4] + moments[4:8] + moments[8:12]


def dot(a, b):
    return jnp.dot(a, b, preferred_element_type=F32)


def half_wave(u):
    x = u * (math.pi / 2)
    y = x * x
    p = -1.0 / 39916800
    for c in (1.0 / 362880, -1.0 / 5040, 1.0 / 120, -1.0 / 6, 1.0):
        p = p * y + c
    return p * x


def kernel(
    shape,
    mm_pos,
    mm_charge,
    mm_tiles,
    feat,
    pos,
    nbr,
    msg_w,
    rad_w,
    out_w,
    read_w,
    mm_out,
    ml_out,
    win_p,
    win_q,
    tiles,
    feat_buf,
    pos_buf,
    nbr_buf,
    msg_v,
    rad_v,
    out_v,
    read_v,
    near_v,
    near_r,
    own_u,
    word_s,
    value_s,
    count_s,
    basis,
    spread,
    weight_s,
    rad_cols,
    stage,
    force_buf,
    local_sem,
    halo_send,
    halo_recv,
    ml_send,
    ml_recv,
    back_send,
    back_recv,
):
    doms, mls = shape
    patches = feat.shape[0]
    atoms = feat.shape[1]
    nbrs = nbr.shape[1]
    psize = mls * atoms
    layers, nb, width = rad_w.shape
    tile_nbrs, tile_count = mm_tiles.shape

    dom = lax.axis_index("dom")
    me = lax.axis_index("ml")
    flat = dom * mls + me
    after = lax.rem(flat + 1, doms * mls)
    before = lax.rem(flat + doms * mls - 1, doms * mls)
    sides = [(before // mls, lax.rem(before, mls)), (after // mls, lax.rem(after, mls))]
    my_patch = lax.rem(me, patches)

    local = [
        pltpu.make_async_copy(mm_pos, win_p.at[1], local_sem.at[0]),
        pltpu.make_async_copy(mm_charge, win_q.at[1], local_sem.at[1]),
        pltpu.make_async_copy(mm_tiles, tiles, local_sem.at[2]),
        pltpu.make_async_copy(msg_w, msg_v, local_sem.at[3]),
        pltpu.make_async_copy(rad_w, rad_v, local_sem.at[4]),
        pltpu.make_async_copy(out_w, out_v, local_sem.at[5]),
        pltpu.make_async_copy(read_w, read_v, local_sem.at[6]),
        pltpu.make_async_copy(nbr.at[my_patch], nbr_buf.at[me], local_sem.at[7]),
        pltpu.make_async_copy(pos, pos_buf.at[me], local_sem.at[8]),
        pltpu.make_async_copy(feat.at[my_patch], feat_buf.at[me], local_sem.at[9]),
    ]
    for copy in local:
        copy.start()

    barrier = pltpu.get_barrier_semaphore()
    for side in sides:
        pl.semaphore_signal(barrier, inc=1, device_id=side, device_id_type=MESH)
    peers = [lax.rem(me + o, mls) for o in range(1, mls)]
    for peer in peers:
        pl.semaphore_signal(barrier, inc=1, device_id=(dom, peer), device_id_type=MESH)
    pl.semaphore_wait(barrier, mls + 1)

    halo = []
    for k, (side, slab) in enumerate(zip(sides, (2, 0))):
        for m, (src, dst) in enumerate(((mm_pos, win_p), (mm_charge, win_q))):
            halo.append(
                pltpu.make_async_remote_copy(
                    src_ref=src,
                    dst_ref=dst.at[slab],
                    send_sem=halo_send.at[2 * k + m],
                    recv_sem=halo_recv.at[2 * k + m],
                    device_id=side,
                    device_id_type=MESH,
                )
            )
    for copy in halo:
        copy.start()
    moves = []
    for m, (src, dst) in enumerate(((nbr, nbr_buf), (pos, pos_buf), (feat, feat_buf))):
        group = []
        for o, peer in enumerate(peers):
            group.append(
                pltpu.make_async_remote_copy(
                    src_ref=src if m == 1 else src.at[lax.rem(peer, patches)],
                    dst_ref=dst.at[me],
                    send_sem=ml_send.at[m, o],
                    recv_sem=ml_recv.at[m, o],
                    device_id=(dom, peer),
                    device_id_type=MESH,
                )
            )
        for copy in group:
            copy.start()
        moves.append(group)

    for copy in local:
        copy.wait()
    center = nb // 2
    step = RADIUS / nb
    factors = [
        math.exp(-2.0 * (step * (n - center)) ** 2) / math.sqrt(nbrs) for n in range(nb)
    ]
    for l in range(layers):
        columns = jnp.concatenate([rad_v[l], jnp.zeros((width - nb, width), F32)], axis=0).T
        for n in range(nb):
            rad_cols[l, n] = jnp.broadcast_to(columns[:, n : n + 1] * factors[n], (width, TILE))
    left = left_factor(win_p[1])
    for t in range(tile_count):
        own_u[t] = left[:, t * TILE : (t + 1) * TILE].T.astype(BF16)

    def near_slab(slab):
        xyz = win_p[slab]
        right = right_factor(xyz)
        rows = moment_rows(xyz, win_q[slab])
        for t in range(tile_count):
            near_v[slab * tile_count + t] = right[:, t * TILE : (t + 1) * TILE]
            near_r[slab * tile_count + t] = rows[:, t * TILE : (t + 1) * TILE]

    near_slab(1)
    for copy in halo:
        copy.wait_recv()
    near_slab(0)
    near_slab(2)

    def mm_tile(t, carry):
        own = own_u[t]
        total = jnp.zeros((16, TILE), F32)
        for c in range(0, tile_nbrs, 2):
            one, two = tiles[c, t], tiles[c + 1, t]
            right = jnp.concatenate([near_v[one], near_v[two]], axis=1)
            rows = jnp.concatenate([near_r[one], near_r[two]], axis=1)
            inverse = lax.rsqrt(dot(own, right))
            cubed = (inverse * inverse * inverse).astype(BF16)
            total = total + lax.dot_general(
                rows, cubed, (((1,), (1,)), ((), ())), preferred_element_type=F32
            )
        at = pl.ds(pl.multiple_of(t * TILE, TILE), TILE)
        sums = folded(total)
        force = win_p[1, :, at] * sums[3:4] - sums[0:3]
        mm_out[:, at] = force * (COULOMB * win_q[1, :, at])
        return carry

    first_half = tile_count // 2
    lax.fori_loop(0, first_half, mm_tile, 0, unroll=True)

    for copy in moves[0] + moves[1]:
        copy.wait_recv()
    listed = jnp.concatenate([nbr_buf[d] for d in range(mls)], axis=1)
    words = psize // 4
    word_s[...] = lax.rem(listed, words)
    value_s[...] = jnp.left_shift(1, 8 * (listed // words))
    xyz = jnp.concatenate([pos_buf[d, :, my_patch, :] for d in range(mls)], axis=1)
    senders = left_factor(xyz).T.astype(BF16)
    receivers = right_factor(xyz)
    rows = moment_rows(xyz, jnp.ones_like(xyz[0:1]))
    for ib in range(psize // TILE):
        at = slice(ib * TILE, (ib + 1) * TILE)
        place = lax.broadcasted_iota(jnp.int32, (words, TILE), 0)
        counts = jnp.zeros((words, TILE), jnp.int32)
        for k in range(nbrs):
            hit = place == word_s[k : k + 1, at]
            counts = counts + jnp.where(hit, value_s[k : k + 1, at], 0)
        count_s[...] = counts
        for b in range(4):
            for c in range(0, words, CHUNK):
                row = b * words + c
                rows_at = slice(row, row + CHUNK)
                count = (jnp.right_shift(count_s[c : c + CHUNK], 8 * b) & 255).astype(F32)
                squared = dot(senders[rows_at], receivers[:, at])
                distance = jnp.minimum(squared * lax.rsqrt(squared), RADIUS)
                wave = half_wave(1.0 - distance * (1.0 / RADIUS))
                weight = count * (wave * wave)
                weight_s[rows_at, at] = weight
                shifted = distance - center * step
                scaled = shifted * (4.0 * step / math.log(2.0))
                middle = weight * jnp.exp2(shifted * shifted * (-2.0 / math.log(2.0)))
                up = jnp.exp2(scaled)
                down = jnp.exp2(-scaled)
                basis[center * psize + row : center * psize + row + CHUNK, at] = middle.astype(BF16)
                value = middle
                for n in range(center + 1, nb):
                    value = value * up
                    basis[n * psize + row : n * psize + row + CHUNK, at] = value.astype(BF16)
                value = middle
                for n in range(center - 1, -1, -1):
                    value = value * down
                    basis[n * psize + row : n * psize + row + CHUNK, at] = value.astype(BF16)

    for copy in moves[2]:
        copy.wait_recv()
    hidden = feat_buf[...].reshape(psize, width).astype(F32).T.astype(BF16)
    for l in range(layers):
        mixed = dot(msg_v[l].astype(F32).T.astype(BF16), hidden).astype(BF16)
        wide = mixed.astype(F32)
        for n in range(nb):
            column = jnp.concatenate([rad_cols[l, n]] * (psize // TILE), axis=1)
            spread[:, n * psize : (n + 1) * psize] = (column * wide).astype(BF16)
        message = dot(spread[...], basis[...])
        active = (message / (1.0 + jnp.exp(-message))).astype(BF16)
        update = dot(out_v[l].astype(F32).T.astype(BF16), active)
        hidden = (hidden.astype(F32) + update).astype(BF16)
    readout = dot(read_v[...].astype(F32).T.astype(BF16), hidden)
    query = readout[:width].astype(BF16)
    key = readout[width:].T.astype(BF16)
    strength = dot(key, query) * weight_s[...] * (1.0 / width)
    strong = strength.astype(BF16)
    weak = (strength - strong.astype(F32)).astype(BF16)
    sums = folded(dot(rows, strong) + dot(rows, weak))
    force = sums[0:3] - xyz * sums[3:4]
    for d in range(mls):
        stage[d] = force[:, d * atoms : (d + 1) * atoms]
    group = me - my_patch
    returns = []
    for o in range(1, patches):
        owner = group + lax.rem(my_patch + o, patches)
        copy = pltpu.make_async_remote_copy(
            src_ref=stage.at[owner],
            dst_ref=force_buf.at[my_patch],
            send_sem=back_send.at[o - 1],
            recv_sem=back_recv.at[o - 1],
            device_id=(dom, owner),
            device_id_type=MESH,
        )
        copy.start()
        returns.append(copy)
    own = pltpu.make_async_copy(stage.at[me], force_buf.at[my_patch], local_sem.at[0])
    own.start()

    lax.fori_loop(first_half, tile_count, mm_tile, 0, unroll=True)

    for copy in halo:
        copy.wait_send()
    for group in moves:
        for copy in group:
            copy.wait_send()
    own.wait()
    for copy in returns:
        copy.wait()
    for p in range(patches):
        ml_out[:, p, :] = force_buf[p]


def on_device(
    shape,
    mm_positions,
    mm_charge,
    mm_tiles,
    ml_feat,
    ml_positions,
    ml_neighbours,
    msg_weight,
    radial_weight,
    out_weight,
    read_weight,
):
    mls = shape[1]
    patches, atoms, width = ml_feat.shape
    nbrs = ml_neighbours.shape[1]
    psize = mls * atoms
    layers, nb, _ = radial_weight.shape
    count = mm_positions.shape[1]
    tile_count = count // TILE
    dma = pltpu.SemaphoreType.DMA
    mm_force, ml_force = pl.pallas_call(
        functools.partial(kernel, shape),
        out_shape=(
            pltpu.VMEM((3, count), F32),
            pltpu.VMEM((3, patches, atoms), F32),
        ),
        in_specs=[ANY] * 10,
        out_specs=(VMEM, VMEM),
        scratch_shapes=[
            pltpu.VMEM((3, 3, count), F32),
            pltpu.VMEM((3, 1, count), F32),
            pltpu.SMEM(mm_tiles.shape[::-1], jnp.int32),
            pltpu.VMEM((mls, atoms, width), BF16),
            pltpu.VMEM((mls, 3, patches, atoms), F32),
            pltpu.VMEM((mls, nbrs, atoms), jnp.int32),
            pltpu.VMEM(msg_weight.shape, BF16),
            pltpu.VMEM(radial_weight.shape, F32),
            pltpu.VMEM(out_weight.shape, BF16),
            pltpu.VMEM(read_weight.shape, BF16),
            pltpu.VMEM((3 * tile_count, 32, TILE), BF16),
            pltpu.VMEM((3 * tile_count, 16, TILE), BF16),
            pltpu.VMEM((tile_count, TILE, 32), BF16),
            pltpu.VMEM((nbrs, psize), jnp.int32),
            pltpu.VMEM((nbrs, psize), jnp.int32),
            pltpu.VMEM((psize // 4, TILE), jnp.int32),
            pltpu.VMEM((nb * psize, psize), BF16),
            pltpu.VMEM((width, nb * psize), BF16),
            pltpu.VMEM((psize, psize), F32),
            pltpu.VMEM((layers, nb, width, TILE), F32),
            pltpu.VMEM((mls, 3, atoms), F32),
            pltpu.VMEM((patches, 3, atoms), F32),
            dma((10,)),
            dma((4,)),
            dma((4,)),
            dma((3, mls)),
            dma((3, mls)),
            dma((patches,)),
            dma((patches,)),
        ],
        compiler_params=pltpu.CompilerParams(
            collective_id=0, has_side_effects=True, vmem_limit_bytes=60 * 1024 * 1024
        ),
        name="force_step",
    )(
        mm_positions,
        mm_charge.reshape(1, count),
        mm_tiles.T,
        ml_feat,
        ml_positions.transpose(1, 0, 2),
        ml_neighbours,
        msg_weight,
        radial_weight,
        out_weight,
        read_weight,
    )
    return mm_force, ml_force.transpose(1, 0, 2)


def solution(mesh):
    shape = (mesh.shape["dom"], mesh.shape["ml"])
    in_specs = (
        P(None, ("dom", "ml")),
        P(("dom", "ml")),
        P(("dom", "ml"), None),
        P("dom", "ml", None),
        P("dom", None, "ml"),
        P("dom", None, "ml"),
        P(),
        P(),
        P(),
        P(),
    )
    out_specs = (P(None, ("dom", "ml")), P("dom", None, "ml"))
    return jax.shard_map(
        functools.partial(on_device, shape),
        mesh=mesh,
        in_specs=in_specs,
        out_specs=out_specs,
        check_vma=False,
    )
```

```python
import functools
import math

import jax
import jax.numpy as jnp
from jax import lax
from jax.experimental import pallas as pl
from jax.experimental.pallas import tpu as pltpu
from jax.sharding import PartitionSpec as P

TILE = 128
RADIUS = 6.0
SOFTEN = 1.0
COULOMB = 0.5
CHUNK = 32
WAVE = (0.261799388, -0.00299057413, 1.02484123e-05, -1.67106067e-08, 1.52995984e-11)
F32 = jnp.float32
BF16 = jnp.bfloat16
MESH = pl.DeviceIdType.MESH
ANY = pl.BlockSpec(memory_space=pl.ANY)
VMEM = pl.BlockSpec(memory_space=pltpu.VMEM)


def split3(x):
    high = x.astype(BF16).astype(F32)
    rest = x - high
    middle = rest.astype(BF16).astype(F32)
    return high, middle, (rest - middle).astype(BF16).astype(F32)


def last_row(shape):
    return lax.broadcasted_iota(jnp.int32, shape, 0) == 3


def left_factor(xyz):
    norm = jnp.sum(xyz * xyz, axis=0, keepdims=True)
    high, middle, low = split3(jnp.concatenate([xyz, norm], axis=0))
    last = last_row(high.shape)
    one = jnp.ones_like(high)
    groups = [
        high,
        jnp.where(last, middle, high),
        jnp.where(last, low, middle),
        jnp.where(last, one, high),
        jnp.where(last, one, low),
        jnp.where(last, one, middle),
        jnp.zeros_like(high),
        jnp.zeros_like(high),
    ]
    return jnp.concatenate(groups, axis=0)


def right_factor(xyz):
    norm = jnp.sum(xyz * xyz, axis=0, keepdims=True) + SOFTEN
    high, middle, low = split3(jnp.concatenate([-2.0 * xyz, norm], axis=0))
    last = last_row(high.shape)
    one = jnp.ones_like(high)
    groups = [
        jnp.where(last, one, high),
        jnp.where(last, one, middle),
        jnp.where(last, one, high),
        low,
        high,
        middle,
        jnp.zeros_like(high),
        jnp.zeros_like(high),
    ]
    return jnp.concatenate(groups, axis=0).astype(BF16)


def moment_rows(xyz, weight):
    rows = jnp.concatenate([xyz * weight, weight], axis=0)
    high, middle, low = split3(rows)
    return jnp.concatenate([high, middle, low, jnp.zeros_like(high)], axis=0).astype(BF16)


def folded(moments):
    return moments[0:4] + moments[4:8] + moments[8:12]


def dot(a, b):
    return jnp.dot(a, b, preferred_element_type=F32)


def half_wave(w):
    y = w * w
    p = WAVE[-1]
    for c in WAVE[-2::-1]:
        p = p * y + c
    return p * w


def kernel(
    shape,
    mm_pos,
    mm_charge,
    mm_tiles,
    feat,
    pos,
    nbr,
    msg_w,
    rad_w,
    out_w,
    read_w,
    mm_out,
    ml_out,
    win_p,
    win_q,
    tiles,
    feat_buf,
    pos_buf,
    nbr_buf,
    msg_v,
    rad_v,
    out_v,
    read_v,
    near_v,
    near_r,
    own_u,
    word_s,
    value_s,
    count_s,
    basis,
    spread,
    weight_s,
    rad_cols,
    stage,
    force_buf,
    local_sem,
    halo_send,
    halo_recv,
    ml_send,
    ml_recv,
    back_send,
    back_recv,
):
    doms, mls = shape
    patches = feat.shape[0]
    atoms = feat.shape[1]
    nbrs = nbr.shape[1]
    psize = mls * atoms
    layers, nb, width = rad_w.shape
    tile_nbrs, tile_count = mm_tiles.shape

    dom = lax.axis_index("dom")
    me = lax.axis_index("ml")
    flat = dom * mls + me
    after = lax.rem(flat + 1, doms * mls)
    before = lax.rem(flat + doms * mls - 1, doms * mls)
    sides = [(before // mls, lax.rem(before, mls)), (after // mls, lax.rem(after, mls))]
    my_patch = lax.rem(me, patches)

    local = [
        pltpu.make_async_copy(mm_pos, win_p.at[1], local_sem.at[0]),
        pltpu.make_async_copy(mm_charge, win_q.at[1], local_sem.at[1]),
        pltpu.make_async_copy(mm_tiles, tiles, local_sem.at[2]),
        pltpu.make_async_copy(msg_w, msg_v, local_sem.at[3]),
        pltpu.make_async_copy(rad_w, rad_v, local_sem.at[4]),
        pltpu.make_async_copy(out_w, out_v, local_sem.at[5]),
        pltpu.make_async_copy(read_w, read_v, local_sem.at[6]),
        pltpu.make_async_copy(nbr.at[my_patch], nbr_buf.at[me], local_sem.at[7]),
        pltpu.make_async_copy(pos, pos_buf.at[me], local_sem.at[8]),
        pltpu.make_async_copy(feat.at[my_patch], feat_buf.at[me], local_sem.at[9]),
    ]
    for copy in local:
        copy.start()

    barrier = pltpu.get_barrier_semaphore()
    for side in sides:
        pl.semaphore_signal(barrier, inc=1, device_id=side, device_id_type=MESH)
    peers = [lax.rem(me + o, mls) for o in range(1, mls)]
    for peer in peers:
        pl.semaphore_signal(barrier, inc=1, device_id=(dom, peer), device_id_type=MESH)
    pl.semaphore_wait(barrier, mls + 1)

    halo = []
    for k, (side, slab) in enumerate(zip(sides, (2, 0))):
        for m, (src, dst) in enumerate(((mm_pos, win_p), (mm_charge, win_q))):
            halo.append(
                pltpu.make_async_remote_copy(
                    src_ref=src,
                    dst_ref=dst.at[slab],
                    send_sem=halo_send.at[2 * k + m],
                    recv_sem=halo_recv.at[2 * k + m],
                    device_id=side,
                    device_id_type=MESH,
                )
            )
    moves = []
    for m, (src, dst) in enumerate(((nbr, nbr_buf), (pos, pos_buf), (feat, feat_buf))):
        group = []
        for o, peer in enumerate(peers):
            group.append(
                pltpu.make_async_remote_copy(
                    src_ref=src if m == 1 else src.at[lax.rem(peer, patches)],
                    dst_ref=dst.at[me],
                    send_sem=ml_send.at[m, o],
                    recv_sem=ml_recv.at[m, o],
                    device_id=(dom, peer),
                    device_id_type=MESH,
                )
            )
        for copy in group:
            copy.start()
        moves.append(group)
    for copy in halo:
        copy.start()

    for copy in local:
        copy.wait()
    center = nb // 2
    step = RADIUS / nb
    factors = [
        math.exp(-2.0 * (step * (n - center)) ** 2) / math.sqrt(nbrs) for n in range(nb)
    ]
    for l in range(layers):
        columns = jnp.concatenate([rad_v[l], jnp.zeros((width - nb, width), F32)], axis=0).T
        for n in range(nb):
            rad_cols[l, n] = jnp.broadcast_to(columns[:, n : n + 1] * factors[n], (width, TILE))
    left = left_factor(win_p[1])
    for t in range(tile_count):
        own_u[t] = left[:, t * TILE : (t + 1) * TILE].T.astype(BF16)

    def near_slab(slab):
        xyz = win_p[slab]
        right = right_factor(xyz)
        rows = moment_rows(xyz, win_q[slab])
        for t in range(tile_count):
            near_v[slab * tile_count + t] = right[:, t * TILE : (t + 1) * TILE]
            near_r[slab * tile_count + t] = rows[:, t * TILE : (t + 1) * TILE]

    near_slab(1)

    def mm_tile(t, carry):
        own = own_u[t]
        total = jnp.zeros((16, TILE), F32)
        for c in range(0, tile_nbrs, 2):
            one, two = tiles[c, t], tiles[c + 1, t]
            right = jnp.concatenate([near_v[one], near_v[two]], axis=1)
            rows = jnp.concatenate([near_r[one], near_r[two]], axis=1)
            inverse = lax.rsqrt(dot(own, right))
            cubed = (inverse * inverse * inverse).astype(BF16)
            total = total + lax.dot_general(
                rows, cubed, (((1,), (1,)), ((), ())), preferred_element_type=F32
            )
        at = pl.ds(pl.multiple_of(t * TILE, TILE), TILE)
        sums = folded(total)
        force = win_p[1, :, at] * sums[3:4] - sums[0:3]
        mm_out[:, at] = force * (COULOMB * win_q[1, :, at])
        return carry

    for copy in moves[0] + moves[1]:
        copy.wait_recv()
    listed = jnp.concatenate([nbr_buf[d] for d in range(mls)], axis=1)
    words = psize // 4
    half = psize // 8
    word_s[...] = lax.rem(listed, half)
    value_s[...] = jnp.left_shift(1, 4 * (listed // half))
    xyz = jnp.concatenate([pos_buf[d, :, my_patch, :] for d in range(mls)], axis=1)
    senders = left_factor(xyz).T.astype(BF16)
    receivers = right_factor(xyz)
    rows = moment_rows(xyz, jnp.ones_like(xyz[0:1]))
    weight_s[...] = dot(senders, receivers)
    for ib in range(psize // TILE):
        at = slice(ib * TILE, (ib + 1) * TILE)
        place = lax.broadcasted_iota(jnp.int32, (words // 2, TILE), 0)
        even = jnp.zeros((words // 2, TILE), jnp.int32)
        odd = even
        for first in range(0, nbrs, 15):
            counts = jnp.zeros((words // 2, TILE), jnp.int32)
            for k in range(first, min(first + 15, nbrs)):
                hit = place == word_s[k : k + 1, at]
                counts = counts + jnp.where(hit, value_s[k : k + 1, at], 0)
            even = even + (counts & 0x0F0F0F0F)
            odd = odd + (jnp.right_shift(counts, 4) & 0x0F0F0F0F)
        count_s[: words // 2] = even
        count_s[words // 2 :] = odd
        for b in range(4):
            for c in range(0, words, CHUNK):
                row = b * words + c
                rows_at = slice(row, row + CHUNK)
                count = (jnp.right_shift(count_s[c : c + CHUNK], 8 * b) & 255).astype(F32)
                squared = weight_s[rows_at, at]
                distance = jnp.minimum(squared * lax.rsqrt(squared), RADIUS)
                wave = half_wave(RADIUS - distance)
                weight = count * (wave * wave)
                weight_s[rows_at, at] = weight
                shifted = distance - center * step
                scaled = shifted * (4.0 * step / math.log(2.0))
                middle = weight * jnp.exp2(shifted * shifted * (-2.0 / math.log(2.0)))
                up = jnp.exp2(scaled)
                down = jnp.exp2(-scaled)
                basis[center * psize + row : center * psize + row + CHUNK, at] = middle.astype(BF16)
                value = middle
                for n in range(center + 1, nb):
                    value = value * up
                    basis[n * psize + row : n * psize + row + CHUNK, at] = value.astype(BF16)
                value = middle
                for n in range(center - 1, -1, -1):
                    value = value * down
                    basis[n * psize + row : n * psize + row + CHUNK, at] = value.astype(BF16)

    for copy in moves[2]:
        copy.wait_recv()
    hidden = feat_buf[...].reshape(psize, width).astype(F32).T.astype(BF16)
    for l in range(layers):
        mixed = dot(msg_v[l].astype(F32).T.astype(BF16), hidden).astype(BF16)
        wide = mixed.astype(F32)
        for n in range(nb):
            column = jnp.concatenate([rad_cols[l, n]] * (psize // TILE), axis=1)
            spread[:, n * psize : (n + 1) * psize] = (column * wide).astype(BF16)
        message = dot(spread[...], basis[...])
        active = (message / (1.0 + jnp.exp(-message))).astype(BF16)
        update = dot(out_v[l].astype(F32).T.astype(BF16), active)
        hidden = (hidden.astype(F32) + update).astype(BF16)
    readout = dot(read_v[...].astype(F32).T.astype(BF16), hidden)
    query = readout[:width].astype(BF16)
    key = readout[width:].T.astype(BF16)
    strength = dot(key, query) * weight_s[...] * (1.0 / width)
    strong = strength.astype(BF16)
    weak = (strength - strong.astype(F32)).astype(BF16)
    sums = folded(dot(rows, strong) + dot(rows, weak))
    force = sums[0:3] - xyz * sums[3:4]
    for d in range(mls):
        stage[d] = force[:, d * atoms : (d + 1) * atoms]
    group = me - my_patch
    returns = []
    for o in range(1, patches):
        owner = group + lax.rem(my_patch + o, patches)
        copy = pltpu.make_async_remote_copy(
            src_ref=stage.at[owner],
            dst_ref=force_buf.at[my_patch],
            send_sem=back_send.at[o - 1],
            recv_sem=back_recv.at[o - 1],
            device_id=(dom, owner),
            device_id_type=MESH,
        )
        copy.start()
        returns.append(copy)
    own = pltpu.make_async_copy(stage.at[me], force_buf.at[my_patch], local_sem.at[0])
    own.start()

    for copy in halo:
        copy.wait_recv()
    near_slab(0)
    near_slab(2)
    lax.fori_loop(0, tile_count, mm_tile, 0, unroll=True)

    for copy in halo:
        copy.wait_send()
    for group in moves:
        for copy in group:
            copy.wait_send()
    own.wait()
    for copy in returns:
        copy.wait()
    for p in range(patches):
        ml_out[:, p, :] = force_buf[p]


def finish(mm_src, ml_src, mm_dst, ml_dst, sem):
    copies = [
        pltpu.make_async_copy(mm_src, mm_dst, sem.at[0]),
        pltpu.make_async_copy(ml_src, ml_dst, sem.at[1]),
    ]
    for copy in copies:
        copy.start()
    for copy in copies:
        copy.wait()


def on_device(
    shape,
    mm_positions,
    mm_charge,
    mm_tiles,
    ml_feat,
    ml_positions,
    ml_neighbours,
    msg_weight,
    radial_weight,
    out_weight,
    read_weight,
):
    mls = shape[1]
    patches, atoms, width = ml_feat.shape
    nbrs = ml_neighbours.shape[1]
    psize = mls * atoms
    layers, nb, _ = radial_weight.shape
    count = mm_positions.shape[1]
    tile_count = count // TILE
    dma = pltpu.SemaphoreType.DMA
    mm_force, ml_force = pl.pallas_call(
        functools.partial(kernel, shape),
        out_shape=(
            pltpu.VMEM((3, count), F32),
            pltpu.VMEM((3, patches, atoms), F32),
        ),
        in_specs=[ANY] * 10,
        out_specs=(VMEM, VMEM),
        scratch_shapes=[
            pltpu.VMEM((3, 3, count), F32),
            pltpu.VMEM((3, 1, count), F32),
            pltpu.SMEM(mm_tiles.shape[::-1], jnp.int32),
            pltpu.VMEM((mls, atoms, width), BF16),
            pltpu.VMEM((mls, 3, patches, atoms), F32),
            pltpu.VMEM((mls, nbrs, atoms), jnp.int32),
            pltpu.VMEM(msg_weight.shape, BF16),
            pltpu.VMEM(radial_weight.shape, F32),
            pltpu.VMEM(out_weight.shape, BF16),
            pltpu.VMEM(read_weight.shape, BF16),
            pltpu.VMEM((3 * tile_count, 32, TILE), BF16),
            pltpu.VMEM((3 * tile_count, 16, TILE), BF16),
            pltpu.VMEM((tile_count, TILE, 32), BF16),
            pltpu.VMEM((nbrs, psize), jnp.int32),
            pltpu.VMEM((nbrs, psize), jnp.int32),
            pltpu.VMEM((psize // 4, TILE), jnp.int32),
            pltpu.VMEM((nb * psize, psize), BF16),
            pltpu.VMEM((width, nb * psize), BF16),
            pltpu.VMEM((psize, psize), F32),
            pltpu.VMEM((layers, nb, width, TILE), F32),
            pltpu.VMEM((mls, 3, atoms), F32),
            pltpu.VMEM((patches, 3, atoms), F32),
            dma((10,)),
            dma((4,)),
            dma((4,)),
            dma((3, mls)),
            dma((3, mls)),
            dma((patches,)),
            dma((patches,)),
        ],
        compiler_params=pltpu.CompilerParams(
            collective_id=0, has_side_effects=True, vmem_limit_bytes=60 * 1024 * 1024
        ),
        name="force_step",
    )(
        mm_positions,
        mm_charge.reshape(1, count),
        mm_tiles.T,
        ml_feat,
        ml_positions.transpose(1, 0, 2),
        ml_neighbours,
        msg_weight,
        radial_weight,
        out_weight,
        read_weight,
    )
    mm_force, ml_force = pl.pallas_call(
        finish,
        out_shape=(
            jax.ShapeDtypeStruct((3, count), F32),
            jax.ShapeDtypeStruct((3, patches, atoms), F32),
        ),
        in_specs=[VMEM, VMEM],
        out_specs=(ANY, ANY),
        scratch_shapes=[dma((2,))],
        name="write_out",
    )(mm_force, ml_force)
    return mm_force, ml_force.transpose(1, 0, 2)


def solution(mesh):
    shape = (mesh.shape["dom"], mesh.shape["ml"])
    in_specs = (
        P(None, ("dom", "ml")),
        P(("dom", "ml")),
        P(("dom", "ml"), None),
        P("dom", "ml", None),
        P("dom", None, "ml"),
        P("dom", None, "ml"),
        P(),
        P(),
        P(),
        P(),
    )
    out_specs = (P(None, ("dom", "ml")), P("dom", None, "ml"))
    return jax.shard_map(
        functools.partial(on_device, shape),
        mesh=mesh,
        in_specs=in_specs,
        out_specs=out_specs,
        check_vma=False,
    )
```

```python
import functools
import math

import jax
import jax.numpy as jnp
from jax import lax
from jax.experimental import pallas as pl
from jax.experimental.pallas import tpu as pltpu
from jax.sharding import PartitionSpec as P

TILE = 128
RADIUS = 6.0
SOFTEN = 1.0
COULOMB = 0.5
CHUNK = 32
WAVE = (0.261799388, -0.00299057413, 1.02484123e-05, -1.67106067e-08, 1.52995984e-11)
F32 = jnp.float32
BF16 = jnp.bfloat16
MESH = pl.DeviceIdType.MESH
ANY = pl.BlockSpec(memory_space=pl.ANY)
VMEM = pl.BlockSpec(memory_space=pltpu.VMEM)


def split3(x):
    high = x.astype(BF16).astype(F32)
    rest = x - high
    middle = rest.astype(BF16).astype(F32)
    return high, middle, (rest - middle).astype(BF16).astype(F32)


def last_row(shape):
    return lax.broadcasted_iota(jnp.int32, shape, 0) == 3


def left_factor(xyz):
    norm = jnp.sum(xyz * xyz, axis=0, keepdims=True)
    high, middle, low = split3(jnp.concatenate([xyz, norm], axis=0))
    last = last_row(high.shape)
    one = jnp.ones_like(high)
    groups = [
        high,
        jnp.where(last, middle, high),
        jnp.where(last, low, middle),
        jnp.where(last, one, high),
        jnp.where(last, one, low),
        jnp.where(last, one, middle),
        jnp.zeros_like(high),
        jnp.zeros_like(high),
    ]
    return jnp.concatenate(groups, axis=0)


def right_factor(xyz):
    norm = jnp.sum(xyz * xyz, axis=0, keepdims=True) + SOFTEN
    high, middle, low = split3(jnp.concatenate([-2.0 * xyz, norm], axis=0))
    last = last_row(high.shape)
    one = jnp.ones_like(high)
    groups = [
        jnp.where(last, one, high),
        jnp.where(last, one, middle),
        jnp.where(last, one, high),
        low,
        high,
        middle,
        jnp.zeros_like(high),
        jnp.zeros_like(high),
    ]
    return jnp.concatenate(groups, axis=0).astype(BF16)


def moment_rows(xyz, weight):
    rows = jnp.concatenate([xyz * weight, weight], axis=0)
    high, middle, low = split3(rows)
    return jnp.concatenate([high, middle, low, jnp.zeros_like(high)], axis=0).astype(BF16)


def folded(moments):
    return moments[0:4] + moments[4:8] + moments[8:12]


def dot(a, b):
    return jnp.dot(a, b, preferred_element_type=F32)


def half_wave(w):
    y = w * w
    p = WAVE[-1]
    for c in WAVE[-2::-1]:
        p = p * y + c
    return p * w


def kernel(
    shape,
    mm_pos,
    mm_charge,
    mm_tiles,
    feat,
    pos,
    nbr,
    msg_w,
    rad_w,
    out_w,
    read_w,
    mm_out,
    ml_out,
    win_p,
    win_q,
    tiles,
    feat_buf,
    nbr_own,
    pos_own,
    geo_own,
    geo_buf,
    msg_v,
    rad_v,
    out_v,
    read_v,
    near_v,
    near_r,
    own_u,
    word_s,
    value_s,
    count_s,
    basis,
    spread,
    weight_s,
    rad_cols,
    stage,
    force_buf,
    local_sem,
    halo_send,
    halo_recv,
    ml_send,
    ml_recv,
    back_send,
    back_recv,
):
    doms, mls = shape
    patches = feat.shape[0]
    atoms = feat.shape[1]
    nbrs = nbr.shape[1]
    psize = mls * atoms
    layers, nb, width = rad_w.shape
    tile_nbrs, tile_count = mm_tiles.shape

    dom = lax.axis_index("dom")
    me = lax.axis_index("ml")
    flat = dom * mls + me
    after = lax.rem(flat + 1, doms * mls)
    before = lax.rem(flat + doms * mls - 1, doms * mls)
    sides = [(before // mls, lax.rem(before, mls)), (after // mls, lax.rem(after, mls))]
    my_patch = lax.rem(me, patches)

    loads = [
        pltpu.make_async_copy(nbr, nbr_own, local_sem.at[7]),
        pltpu.make_async_copy(pos, pos_own, local_sem.at[8]),
    ]
    local = [
        pltpu.make_async_copy(mm_pos, win_p.at[1], local_sem.at[0]),
        pltpu.make_async_copy(mm_charge, win_q.at[1], local_sem.at[1]),
        pltpu.make_async_copy(mm_tiles, tiles, local_sem.at[2]),
        pltpu.make_async_copy(msg_w, msg_v, local_sem.at[3]),
        pltpu.make_async_copy(rad_w, rad_v, local_sem.at[4]),
        pltpu.make_async_copy(out_w, out_v, local_sem.at[5]),
        pltpu.make_async_copy(read_w, read_v, local_sem.at[6]),
        pltpu.make_async_copy(feat.at[my_patch], feat_buf.at[me], local_sem.at[9]),
    ]
    for copy in loads + local:
        copy.start()

    barrier = pltpu.get_barrier_semaphore()
    for side in sides:
        pl.semaphore_signal(barrier, inc=1, device_id=side, device_id_type=MESH)
    peers = [lax.rem(me + o, mls) for o in range(1, mls)]
    for peer in peers:
        pl.semaphore_signal(barrier, inc=1, device_id=(dom, peer), device_id_type=MESH)

    for copy in loads:
        copy.wait()
    quarter = nbrs // 4
    assert nbrs % 4 == 0 and psize & (psize - 1) == 0 and psize <= 4096
    for p in range(patches):
        pairs = nbr_own[p, : 2 * quarter] + psize * nbr_own[p, 2 * quarter :]
        pairs = jnp.concatenate([pairs[:quarter], pairs[quarter:]], axis=1)
        geo_own[p, :quarter] = pairs.astype(F32)
        geo_own[p, quarter : quarter + 3, :atoms] = pos_own[:, p, :]
        geo_own[p, quarter : quarter + 3, atoms:] = pos_own[:, p, :]
        geo_own[p, quarter + 3 :] = jnp.zeros((geo_own.shape[1] - quarter - 3, 2 * atoms), F32)

    pl.semaphore_wait(barrier, mls + 1)

    halo = []
    for k, (side, slab) in enumerate(zip(sides, (2, 0))):
        for m, (src, dst) in enumerate(((mm_pos, win_p), (mm_charge, win_q))):
            halo.append(
                pltpu.make_async_remote_copy(
                    src_ref=src,
                    dst_ref=dst.at[slab],
                    send_sem=halo_send.at[2 * k + m],
                    recv_sem=halo_recv.at[2 * k + m],
                    device_id=side,
                    device_id_type=MESH,
                )
            )
    moves = []
    for m, (src, dst) in enumerate(((geo_own, geo_buf), (feat, feat_buf))):
        group = []
        for o, peer in enumerate(peers):
            group.append(
                pltpu.make_async_remote_copy(
                    src_ref=src.at[lax.rem(peer, patches)],
                    dst_ref=dst.at[me],
                    send_sem=ml_send.at[m, o],
                    recv_sem=ml_recv.at[m, o],
                    device_id=(dom, peer),
                    device_id_type=MESH,
                )
            )
        for copy in group:
            copy.start()
        moves.append(group)
    for copy in halo:
        copy.start()

    geo_buf[me] = geo_own[my_patch]
    for copy in local:
        copy.wait()
    center = nb // 2
    step = RADIUS / nb
    factors = [
        math.exp(-2.0 * (step * (n - center)) ** 2) / math.sqrt(nbrs) for n in range(nb)
    ]
    for l in range(layers):
        columns = jnp.concatenate([rad_v[l], jnp.zeros((width - nb, width), F32)], axis=0).T
        for n in range(nb):
            rad_cols[l, n] = jnp.broadcast_to(columns[:, n : n + 1] * factors[n], (width, TILE))
    left = left_factor(win_p[1])
    for t in range(tile_count):
        own_u[t] = left[:, t * TILE : (t + 1) * TILE].T.astype(BF16)

    def near_slab(slab):
        xyz = win_p[slab]
        right = right_factor(xyz)
        rows = moment_rows(xyz, win_q[slab])
        for t in range(tile_count):
            near_v[slab * tile_count + t] = right[:, t * TILE : (t + 1) * TILE]
            near_r[slab * tile_count + t] = rows[:, t * TILE : (t + 1) * TILE]

    near_slab(1)

    def mm_tile(t, carry):
        own = own_u[t]
        total = jnp.zeros((16, TILE), F32)
        for c in range(0, tile_nbrs, 2):
            one, two = tiles[c, t], tiles[c + 1, t]
            right = jnp.concatenate([near_v[one], near_v[two]], axis=1)
            rows = jnp.concatenate([near_r[one], near_r[two]], axis=1)
            inverse = lax.rsqrt(dot(own, right))
            cubed = (inverse * inverse * inverse).astype(BF16)
            total = total + lax.dot_general(
                rows, cubed, (((1,), (1,)), ((), ())), preferred_element_type=F32
            )
        at = pl.ds(pl.multiple_of(t * TILE, TILE), TILE)
        sums = folded(total)
        force = win_p[1, :, at] * sums[3:4] - sums[0:3]
        mm_out[:, at] = force * (COULOMB * win_q[1, :, at])
        return carry

    for copy in moves[0]:
        copy.wait_recv()
    pieces = [geo_buf[d] for d in range(mls)]
    pairs = jnp.concatenate(
        [
            jnp.concatenate([piece[:quarter, :atoms] for piece in pieces], axis=1),
            jnp.concatenate([piece[:quarter, atoms:] for piece in pieces], axis=1),
        ],
        axis=0,
    ).astype(jnp.int32)
    bits = psize.bit_length() - 1
    listed = jnp.concatenate([pairs & (psize - 1), jnp.right_shift(pairs, bits)], axis=0)
    words = psize // 4
    half = psize // 8
    word_s[...] = listed & (half - 1)
    value_s[...] = jnp.left_shift(1, 4 * jnp.right_shift(listed, bits - 3))
    xyz = jnp.concatenate([piece[quarter : quarter + 3, :atoms] for piece in pieces], axis=1)
    senders = left_factor(xyz).T.astype(BF16)
    receivers = right_factor(xyz)
    rows = moment_rows(xyz, jnp.ones_like(xyz[0:1]))
    weight_s[...] = dot(senders, receivers)
    for ib in range(psize // TILE):
        at = slice(ib * TILE, (ib + 1) * TILE)
        place = lax.broadcasted_iota(jnp.int32, (words // 2, TILE), 0)
        even = jnp.zeros((words // 2, TILE), jnp.int32)
        odd = even
        for first in range(0, nbrs, 15):
            counts = jnp.zeros((words // 2, TILE), jnp.int32)
            for k in range(first, min(first + 15, nbrs)):
                hit = place == word_s[k : k + 1, at]
                counts = counts + jnp.where(hit, value_s[k : k + 1, at], 0)
            even = even + (counts & 0x0F0F0F0F)
            odd = odd + (jnp.right_shift(counts, 4) & 0x0F0F0F0F)
        count_s[: words // 2] = even
        count_s[words // 2 :] = odd
        for b in range(4):
            for c in range(0, words, CHUNK):
                row = b * words + c
                rows_at = slice(row, row + CHUNK)
                count = (jnp.right_shift(count_s[c : c + CHUNK], 8 * b) & 255).astype(F32)
                squared = weight_s[rows_at, at]
                distance = jnp.minimum(squared * lax.rsqrt(squared), RADIUS)
                wave = half_wave(RADIUS - distance)
                weight = count * (wave * wave)
                weight_s[rows_at, at] = weight
                shifted = distance - center * step
                scaled = shifted * (4.0 * step / math.log(2.0))
                middle = weight * jnp.exp2(shifted * shifted * (-2.0 / math.log(2.0)))
                up = jnp.exp2(scaled)
                down = jnp.exp2(-scaled)
                basis[center * psize + row : center * psize + row + CHUNK, at] = middle.astype(BF16)
                value = middle
                for n in range(center + 1, nb):
                    value = value * up
                    basis[n * psize + row : n * psize + row + CHUNK, at] = value.astype(BF16)
                value = middle
                for n in range(center - 1, -1, -1):
                    value = value * down
                    basis[n * psize + row : n * psize + row + CHUNK, at] = value.astype(BF16)

    for copy in moves[1]:
        copy.wait_recv()
    hidden = feat_buf[...].reshape(psize, width).astype(F32).T.astype(BF16)
    for l in range(layers):
        mixed = dot(msg_v[l].astype(F32).T.astype(BF16), hidden).astype(BF16)
        wide = mixed.astype(F32)
        for n in range(nb):
            column = jnp.concatenate([rad_cols[l, n]] * (psize // TILE), axis=1)
            spread[:, n * psize : (n + 1) * psize] = (column * wide).astype(BF16)
        message = dot(spread[...], basis[...])
        active = (message / (1.0 + jnp.exp(-message))).astype(BF16)
        update = dot(out_v[l].astype(F32).T.astype(BF16), active)
        hidden = (hidden.astype(F32) + update).astype(BF16)
    readout = dot(read_v[...].astype(F32).T.astype(BF16), hidden)
    query = readout[:width].astype(BF16)
    key = readout[width:].T.astype(BF16)
    strength = dot(key, query) * weight_s[...] * (1.0 / width)
    strong = strength.astype(BF16)
    weak = (strength - strong.astype(F32)).astype(BF16)
    sums = folded(dot(rows, strong) + dot(rows, weak))
    force = sums[0:3] - xyz * sums[3:4]
    for d in range(mls):
        stage[d] = force[:, d * atoms : (d + 1) * atoms]
    group = me - my_patch
    returns = []
    for o in range(1, patches):
        owner = group + lax.rem(my_patch + o, patches)
        copy = pltpu.make_async_remote_copy(
            src_ref=stage.at[owner],
            dst_ref=force_buf.at[my_patch],
            send_sem=back_send.at[o - 1],
            recv_sem=back_recv.at[o - 1],
            device_id=(dom, owner),
            device_id_type=MESH,
        )
        copy.start()
        returns.append(copy)
    own = pltpu.make_async_copy(stage.at[me], force_buf.at[my_patch], local_sem.at[0])
    own.start()

    for copy in halo:
        copy.wait_recv()
    near_slab(0)
    near_slab(2)
    lax.fori_loop(0, tile_count, mm_tile, 0, unroll=True)

    for copy in halo:
        copy.wait_send()
    for group in moves:
        for copy in group:
            copy.wait_send()
    own.wait()
    for copy in returns:
        copy.wait()
    for p in range(patches):
        ml_out[:, p, :] = force_buf[p]


def on_device(
    shape,
    mm_positions,
    mm_charge,
    mm_tiles,
    ml_feat,
    ml_positions,
    ml_neighbours,
    msg_weight,
    radial_weight,
    out_weight,
    read_weight,
):
    mls = shape[1]
    patches, atoms, width = ml_feat.shape
    nbrs = ml_neighbours.shape[1]
    psize = mls * atoms
    layers, nb, _ = radial_weight.shape
    count = mm_positions.shape[1]
    tile_count = count // TILE
    dma = pltpu.SemaphoreType.DMA
    geo_rows = (nbrs // 4 + 3 + 7) // 8 * 8
    mm_force, ml_force = pl.pallas_call(
        functools.partial(kernel, shape),
        out_shape=(
            pltpu.VMEM((3, count), F32),
            pltpu.VMEM((3, patches, atoms), F32),
        ),
        in_specs=[ANY] * 10,
        out_specs=(VMEM, VMEM),
        scratch_shapes=[
            pltpu.VMEM((3, 3, count), F32),
            pltpu.VMEM((3, 1, count), F32),
            pltpu.SMEM(mm_tiles.shape[::-1], jnp.int32),
            pltpu.VMEM((mls, atoms, width), BF16),
            pltpu.VMEM((patches, nbrs, atoms), jnp.int32),
            pltpu.VMEM((3, patches, atoms), F32),
            pltpu.VMEM((patches, geo_rows, 2 * atoms), F32),
            pltpu.VMEM((mls, geo_rows, 2 * atoms), F32),
            pltpu.VMEM(msg_weight.shape, BF16),
            pltpu.VMEM(radial_weight.shape, F32),
            pltpu.VMEM(out_weight.shape, BF16),
            pltpu.VMEM(read_weight.shape, BF16),
            pltpu.VMEM((3 * tile_count, 32, TILE), BF16),
            pltpu.VMEM((3 * tile_count, 16, TILE), BF16),
            pltpu.VMEM((tile_count, TILE, 32), BF16),
            pltpu.VMEM((nbrs, psize), jnp.int32),
            pltpu.VMEM((nbrs, psize), jnp.int32),
            pltpu.VMEM((psize // 4, TILE), jnp.int32),
            pltpu.VMEM((nb * psize, psize), BF16),
            pltpu.VMEM((width, nb * psize), BF16),
            pltpu.VMEM((psize, psize), F32),
            pltpu.VMEM((layers, nb, width, TILE), F32),
            pltpu.VMEM((mls, 3, atoms), F32),
            pltpu.VMEM((patches, 3, atoms), F32),
            dma((10,)),
            dma((4,)),
            dma((4,)),
            dma((2, mls)),
            dma((2, mls)),
            dma((patches,)),
            dma((patches,)),
        ],
        compiler_params=pltpu.CompilerParams(
            collective_id=0, has_side_effects=True, vmem_limit_bytes=60 * 1024 * 1024
        ),
        name="force_step",
    )(
        mm_positions,
        mm_charge.reshape(1, count),
        mm_tiles.T,
        ml_feat,
        ml_positions.transpose(1, 0, 2),
        ml_neighbours,
        msg_weight,
        radial_weight,
        out_weight,
        read_weight,
    )
    return mm_force, ml_force.transpose(1, 0, 2)


def solution(mesh):
    shape = (mesh.shape["dom"], mesh.shape["ml"])
    in_specs = (
        P(None, ("dom", "ml")),
        P(("dom", "ml")),
        P(("dom", "ml"), None),
        P("dom", "ml", None),
        P("dom", None, "ml"),
        P("dom", None, "ml"),
        P(),
        P(),
        P(),
        P(),
    )
    out_specs = (P(None, ("dom", "ml")), P("dom", None, "ml"))
    return jax.shard_map(
        functools.partial(on_device, shape),
        mesh=mesh,
        in_specs=in_specs,
        out_specs=out_specs,
        check_vma=False,
    )
```

```python
import functools
import math

import jax
import jax.numpy as jnp
from jax import lax
from jax.experimental import pallas as pl
from jax.experimental.pallas import tpu as pltpu
from jax.sharding import PartitionSpec as P

TILE = 128
RADIUS = 6.0
SOFTEN = 1.0
COULOMB = 0.5
CHUNK = 32
WAVE = (0.261799388, -0.00299057413, 1.02484123e-05, -1.67106067e-08, 1.52995984e-11)
F32 = jnp.float32
BF16 = jnp.bfloat16
MESH = pl.DeviceIdType.MESH
ANY = pl.BlockSpec(memory_space=pl.ANY)
VMEM = pl.BlockSpec(memory_space=pltpu.VMEM)


def split3(x):
    high = x.astype(BF16).astype(F32)
    rest = x - high
    middle = rest.astype(BF16).astype(F32)
    return high, middle, (rest - middle).astype(BF16).astype(F32)


def last_row(shape):
    return lax.broadcasted_iota(jnp.int32, shape, 0) == 3


def left_factor(xyz):
    norm = jnp.sum(xyz * xyz, axis=0, keepdims=True)
    high, middle, low = split3(jnp.concatenate([xyz, norm], axis=0))
    last = last_row(high.shape)
    one = jnp.ones_like(high)
    groups = [
        high,
        jnp.where(last, middle, high),
        jnp.where(last, low, middle),
        jnp.where(last, one, high),
        jnp.where(last, one, low),
        jnp.where(last, one, middle),
        jnp.zeros_like(high),
        jnp.zeros_like(high),
    ]
    return jnp.concatenate(groups, axis=0)


def right_factor(xyz):
    norm = jnp.sum(xyz * xyz, axis=0, keepdims=True) + SOFTEN
    high, middle, low = split3(jnp.concatenate([-2.0 * xyz, norm], axis=0))
    last = last_row(high.shape)
    one = jnp.ones_like(high)
    groups = [
        jnp.where(last, one, high),
        jnp.where(last, one, middle),
        jnp.where(last, one, high),
        low,
        high,
        middle,
        jnp.zeros_like(high),
        jnp.zeros_like(high),
    ]
    return jnp.concatenate(groups, axis=0).astype(BF16)


def moment_rows(xyz, weight):
    rows = jnp.concatenate([xyz * weight, weight], axis=0)
    high, middle, low = split3(rows)
    return jnp.concatenate([high, middle, low, jnp.zeros_like(high)], axis=0).astype(BF16)


def folded(moments):
    return moments[0:4] + moments[4:8] + moments[8:12]


def dot(a, b):
    return jnp.dot(a, b, preferred_element_type=F32)


def half_wave(w):
    y = w * w
    p = WAVE[-1]
    for c in WAVE[-2::-1]:
        p = p * y + c
    return p * w


def kernel(
    shape,
    mm_pos,
    mm_charge,
    mm_tiles,
    feat,
    pos,
    nbr,
    msg_w,
    rad_w,
    out_w,
    read_w,
    mm_out,
    ml_out,
    win_p,
    win_q,
    tiles,
    feat_buf,
    nbr_own,
    pos_own,
    geo_own,
    geo_buf,
    msg_v,
    rad_v,
    out_v,
    read_v,
    turned,
    read_t,
    near_v,
    near_r,
    own_u,
    word_s,
    value_s,
    count_s,
    basis,
    spread,
    weight_s,
    rad_cols,
    stage,
    force_buf,
    local_sem,
    halo_send,
    halo_recv,
    ml_send,
    ml_recv,
    back_send,
    back_recv,
    all_in,
):
    doms, mls = shape
    patches = feat.shape[0]
    atoms = feat.shape[1]
    nbrs = nbr.shape[1]
    psize = mls * atoms
    layers, nb, width = rad_w.shape
    tile_nbrs, tile_count = mm_tiles.shape

    dom = lax.axis_index("dom")
    me = lax.axis_index("ml")
    flat = dom * mls + me
    after = lax.rem(flat + 1, doms * mls)
    before = lax.rem(flat + doms * mls - 1, doms * mls)
    sides = [(before // mls, lax.rem(before, mls)), (after // mls, lax.rem(after, mls))]
    my_patch = lax.rem(me, patches)

    loads = [
        pltpu.make_async_copy(nbr, nbr_own, local_sem.at[7]),
        pltpu.make_async_copy(pos, pos_own, local_sem.at[8]),
    ]
    local = [
        pltpu.make_async_copy(mm_pos, win_p.at[1], local_sem.at[0]),
        pltpu.make_async_copy(mm_charge, win_q.at[1], local_sem.at[1]),
        pltpu.make_async_copy(mm_tiles, tiles, local_sem.at[2]),
        pltpu.make_async_copy(msg_w, msg_v, local_sem.at[3]),
        pltpu.make_async_copy(rad_w, rad_v, local_sem.at[4]),
        pltpu.make_async_copy(out_w, out_v, local_sem.at[5]),
        pltpu.make_async_copy(read_w, read_v, local_sem.at[6]),
        pltpu.make_async_copy(feat.at[my_patch], feat_buf.at[me], local_sem.at[9]),
    ]
    for copy in loads + local:
        copy.start()

    barrier = pltpu.get_barrier_semaphore()
    low, high = me == 0, me == mls - 1
    edge = low | high
    for target in range(1, mls - 1):

        @pl.when(me != target)
        def _():
            pl.semaphore_signal(barrier, inc=1, device_id=(dom, target), device_id_type=MESH)

    for at_edge, side in zip((low, high), sides):

        @pl.when(at_edge)
        def _():
            pl.semaphore_signal(barrier, inc=1, device_id=side, device_id_type=MESH)

    peers = [lax.rem(me + o, mls) for o in range(1, mls)]

    for copy in loads:
        copy.wait()
    quarter = nbrs // 4
    assert nbrs % 4 == 0 and psize & (psize - 1) == 0 and psize <= 4096
    for p in range(patches):
        pairs = nbr_own[p, : 2 * quarter] + psize * nbr_own[p, 2 * quarter :]
        pairs = jnp.concatenate([pairs[:quarter], pairs[quarter:]], axis=1)
        geo_own[p, :quarter] = pairs.astype(F32)
        geo_own[p, quarter : quarter + 3, :atoms] = pos_own[:, p, :]
        geo_own[p, quarter : quarter + 3, atoms:] = pos_own[:, p, :]
        geo_own[p, quarter + 3 :] = jnp.zeros((geo_own.shape[1] - quarter - 3, 2 * atoms), F32)

    @pl.when(jnp.logical_not(edge))
    def _():
        pl.semaphore_wait(barrier, mls - 1)

    for inner, outer in ((1, 0), (mls - 2, mls - 1)):

        @pl.when(me == inner)
        def _():
            pl.semaphore_signal(all_in, inc=1, device_id=(dom, outer), device_id_type=MESH)

    @pl.when(edge)
    def _():
        pl.semaphore_wait(all_in, 1)


    halo = []
    for k, (side, slab) in enumerate(zip(sides, (2, 0))):
        for m, (src, dst) in enumerate(((mm_pos, win_p), (mm_charge, win_q))):
            halo.append(
                pltpu.make_async_remote_copy(
                    src_ref=src,
                    dst_ref=dst.at[slab],
                    send_sem=halo_send.at[2 * k + m],
                    recv_sem=halo_recv.at[2 * k + m],
                    device_id=side,
                    device_id_type=MESH,
                )
            )
    moves = []
    for m, (src, dst) in enumerate(((geo_own, geo_buf), (feat, feat_buf))):
        group = []
        for o, peer in enumerate(peers):
            group.append(
                pltpu.make_async_remote_copy(
                    src_ref=src.at[lax.rem(peer, patches)],
                    dst_ref=dst.at[me],
                    send_sem=ml_send.at[m, o],
                    recv_sem=ml_recv.at[m, o],
                    device_id=(dom, peer),
                    device_id_type=MESH,
                )
            )
        for copy in group:
            copy.start()
        moves.append(group)
    for k, at_edge in enumerate((low, high)):

        @pl.when(jnp.logical_not(at_edge))
        def _():
            for copy in halo[2 * k : 2 * k + 2]:
                copy.start()


    geo_buf[me] = geo_own[my_patch]
    for copy in local:
        copy.wait()
    for l in range(layers):
        turned[l] = msg_v[l].astype(F32).T.astype(BF16)
        turned[layers + l] = out_v[l].astype(F32).T.astype(BF16)
    read_t[...] = read_v[...].astype(F32).T.astype(BF16)
    center = nb // 2
    step = RADIUS / nb
    factors = [
        math.exp(-2.0 * (step * (n - center)) ** 2) / math.sqrt(nbrs) for n in range(nb)
    ]
    for l in range(layers):
        columns = jnp.concatenate([rad_v[l], jnp.zeros((width - nb, width), F32)], axis=0).T
        for n in range(nb):
            rad_cols[l, n] = jnp.broadcast_to(columns[:, n : n + 1] * factors[n], (width, TILE))
    left = left_factor(win_p[1])
    for t in range(tile_count):
        own_u[t] = left[:, t * TILE : (t + 1) * TILE].T.astype(BF16)

    def near_slab(slab):
        xyz = win_p[slab]
        right = right_factor(xyz)
        rows = moment_rows(xyz, win_q[slab])
        for t in range(tile_count):
            near_v[slab * tile_count + t] = right[:, t * TILE : (t + 1) * TILE]
            near_r[slab * tile_count + t] = rows[:, t * TILE : (t + 1) * TILE]

    near_slab(1)

    def mm_tile(t, carry):
        own = own_u[t]
        total = jnp.zeros((16, TILE), F32)
        for c in range(0, tile_nbrs, 2):
            one, two = tiles[c, t], tiles[c + 1, t]
            right = jnp.concatenate([near_v[one], near_v[two]], axis=1)
            rows = jnp.concatenate([near_r[one], near_r[two]], axis=1)
            inverse = lax.rsqrt(dot(own, right))
            cubed = (inverse * inverse * inverse).astype(BF16)
            total = total + lax.dot_general(
                rows, cubed, (((1,), (1,)), ((), ())), preferred_element_type=F32
            )
        at = pl.ds(pl.multiple_of(t * TILE, TILE), TILE)
        sums = folded(total)
        force = win_p[1, :, at] * sums[3:4] - sums[0:3]
        mm_out[:, at] = force * (COULOMB * win_q[1, :, at])
        return carry

    for copy in moves[0]:
        copy.wait_recv()
    pieces = [geo_buf[d] for d in range(mls)]
    pairs = jnp.concatenate(
        [
            jnp.concatenate([piece[:quarter, :atoms] for piece in pieces], axis=1),
            jnp.concatenate([piece[:quarter, atoms:] for piece in pieces], axis=1),
        ],
        axis=0,
    ).astype(jnp.int32)
    bits = psize.bit_length() - 1
    listed = jnp.concatenate([pairs & (psize - 1), jnp.right_shift(pairs, bits)], axis=0)
    words = psize // 4
    half = psize // 8
    word_s[...] = listed & (half - 1)
    value_s[...] = jnp.left_shift(1, 4 * jnp.right_shift(listed, bits - 3))
    xyz = jnp.concatenate([piece[quarter : quarter + 3, :atoms] for piece in pieces], axis=1)
    senders = left_factor(xyz).T.astype(BF16)
    receivers = right_factor(xyz)
    rows = moment_rows(xyz, jnp.ones_like(xyz[0:1]))
    weight_s[...] = dot(senders, receivers)
    for ib in range(psize // TILE):
        at = slice(ib * TILE, (ib + 1) * TILE)
        place = lax.broadcasted_iota(jnp.int32, (words // 2, TILE), 0)
        even = jnp.zeros((words // 2, TILE), jnp.int32)
        odd = even
        for first in range(0, nbrs, 15):
            counts = jnp.zeros((words // 2, TILE), jnp.int32)
            for k in range(first, min(first + 15, nbrs)):
                hit = place == word_s[k : k + 1, at]
                counts = counts + jnp.where(hit, value_s[k : k + 1, at], 0)
            even = even + (counts & 0x0F0F0F0F)
            odd = odd + (jnp.right_shift(counts, 4) & 0x0F0F0F0F)
        count_s[: words // 2] = even
        count_s[words // 2 :] = odd
        for b in range(4):
            for c in range(0, words, CHUNK):
                row = b * words + c
                rows_at = slice(row, row + CHUNK)
                count = (jnp.right_shift(count_s[c : c + CHUNK], 8 * b) & 255).astype(F32)
                squared = weight_s[rows_at, at]
                distance = jnp.minimum(squared * lax.rsqrt(squared), RADIUS)
                wave = half_wave(RADIUS - distance)
                weight = count * (wave * wave)
                weight_s[rows_at, at] = weight
                shifted = distance - center * step
                scaled = shifted * (4.0 * step / math.log(2.0))
                middle = weight * jnp.exp2(shifted * shifted * (-2.0 / math.log(2.0)))
                up = jnp.exp2(scaled)
                down = jnp.exp2(-scaled)
                basis[center * psize + row : center * psize + row + CHUNK, at] = middle.astype(BF16)
                value = middle
                for n in range(center + 1, nb):
                    value = value * up
                    basis[n * psize + row : n * psize + row + CHUNK, at] = value.astype(BF16)
                value = middle
                for n in range(center - 1, -1, -1):
                    value = value * down
                    basis[n * psize + row : n * psize + row + CHUNK, at] = value.astype(BF16)

    @pl.when(edge)
    def _():
        pl.semaphore_wait(barrier, 1)

    for k, at_edge in enumerate((low, high)):

        @pl.when(at_edge)
        def _():
            for copy in halo[2 * k : 2 * k + 2]:
                copy.start()

    for copy in moves[1]:
        copy.wait_recv()
    hidden = feat_buf[...].reshape(psize, width).astype(F32).T.astype(BF16)
    for l in range(layers):
        mixed = dot(turned[l], hidden).astype(BF16)
        wide = mixed.astype(F32)
        for n in range(nb):
            column = jnp.concatenate([rad_cols[l, n]] * (psize // TILE), axis=1)
            spread[:, n * psize : (n + 1) * psize] = (column * wide).astype(BF16)
        message = dot(spread[...], basis[...])
        active = (message / (1.0 + jnp.exp(-message))).astype(BF16)
        update = dot(turned[layers + l], active)
        hidden = (hidden.astype(F32) + update).astype(BF16)
    readout = dot(read_t[...], hidden)
    query = readout[:width].astype(BF16)
    key = readout[width:].T.astype(BF16)
    strength = dot(key, query) * weight_s[...] * (1.0 / width)
    strong = strength.astype(BF16)
    weak = (strength - strong.astype(F32)).astype(BF16)
    sums = folded(dot(rows, strong) + dot(rows, weak))
    force = sums[0:3] - xyz * sums[3:4]
    for d in range(mls):
        stage[d] = force[:, d * atoms : (d + 1) * atoms]
    group = me - my_patch
    returns = []
    for o in range(1, patches):
        owner = group + lax.rem(my_patch + o, patches)
        copy = pltpu.make_async_remote_copy(
            src_ref=stage.at[owner],
            dst_ref=force_buf.at[my_patch],
            send_sem=back_send.at[o - 1],
            recv_sem=back_recv.at[o - 1],
            device_id=(dom, owner),
            device_id_type=MESH,
        )
        copy.start()
        returns.append(copy)
    own = pltpu.make_async_copy(stage.at[me], force_buf.at[my_patch], local_sem.at[0])
    own.start()

    for copy in halo:
        copy.wait_recv()
    near_slab(0)
    near_slab(2)
    lax.fori_loop(0, tile_count, mm_tile, 0, unroll=True)

    for copy in halo:
        copy.wait_send()
    for group in moves:
        for copy in group:
            copy.wait_send()
    own.wait()
    for copy in returns:
        copy.wait()
    for p in range(patches):
        ml_out[:, p, :] = force_buf[p]


def on_device(
    shape,
    mm_positions,
    mm_charge,
    mm_tiles,
    ml_feat,
    ml_positions,
    ml_neighbours,
    msg_weight,
    radial_weight,
    out_weight,
    read_weight,
):
    mls = shape[1]
    patches, atoms, width = ml_feat.shape
    nbrs = ml_neighbours.shape[1]
    psize = mls * atoms
    layers, nb, _ = radial_weight.shape
    count = mm_positions.shape[1]
    tile_count = count // TILE
    dma = pltpu.SemaphoreType.DMA
    geo_rows = (nbrs // 4 + 3 + 7) // 8 * 8
    mm_force, ml_force = pl.pallas_call(
        functools.partial(kernel, shape),
        out_shape=(
            pltpu.VMEM((3, count), F32),
            pltpu.VMEM((3, patches, atoms), F32),
        ),
        in_specs=[ANY] * 10,
        out_specs=(VMEM, VMEM),
        scratch_shapes=[
            pltpu.VMEM((3, 3, count), F32),
            pltpu.VMEM((3, 1, count), F32),
            pltpu.SMEM(mm_tiles.shape[::-1], jnp.int32),
            pltpu.VMEM((mls, atoms, width), BF16),
            pltpu.VMEM((patches, nbrs, atoms), jnp.int32),
            pltpu.VMEM((3, patches, atoms), F32),
            pltpu.VMEM((patches, geo_rows, 2 * atoms), F32),
            pltpu.VMEM((mls, geo_rows, 2 * atoms), F32),
            pltpu.VMEM(msg_weight.shape, BF16),
            pltpu.VMEM(radial_weight.shape, F32),
            pltpu.VMEM(out_weight.shape, BF16),
            pltpu.VMEM(read_weight.shape, BF16),
            pltpu.VMEM((2 * layers, width, width), BF16),
            pltpu.VMEM(read_weight.shape[::-1], BF16),
            pltpu.VMEM((3 * tile_count, 32, TILE), BF16),
            pltpu.VMEM((3 * tile_count, 16, TILE), BF16),
            pltpu.VMEM((tile_count, TILE, 32), BF16),
            pltpu.VMEM((nbrs, psize), jnp.int32),
            pltpu.VMEM((nbrs, psize), jnp.int32),
            pltpu.VMEM((psize // 4, TILE), jnp.int32),
            pltpu.VMEM((nb * psize, psize), BF16),
            pltpu.VMEM((width, nb * psize), BF16),
            pltpu.VMEM((psize, psize), F32),
            pltpu.VMEM((layers, nb, width, TILE), F32),
            pltpu.VMEM((mls, 3, atoms), F32),
            pltpu.VMEM((patches, 3, atoms), F32),
            dma((10,)),
            dma((4,)),
            dma((4,)),
            dma((2, mls)),
            dma((2, mls)),
            dma((patches,)),
            dma((patches,)),
            pltpu.SemaphoreType.REGULAR,
        ],
        compiler_params=pltpu.CompilerParams(
            collective_id=0, has_side_effects=True, vmem_limit_bytes=60 * 1024 * 1024
        ),
        name="force_step",
    )(
        mm_positions,
        mm_charge.reshape(1, count),
        mm_tiles.T,
        ml_feat,
        ml_positions.transpose(1, 0, 2),
        ml_neighbours,
        msg_weight,
        radial_weight,
        out_weight,
        read_weight,
    )
    return mm_force, ml_force.transpose(1, 0, 2)


def solution(mesh):
    shape = (mesh.shape["dom"], mesh.shape["ml"])
    in_specs = (
        P(None, ("dom", "ml")),
        P(("dom", "ml")),
        P(("dom", "ml"), None),
        P("dom", "ml", None),
        P("dom", None, "ml"),
        P("dom", None, "ml"),
        P(),
        P(),
        P(),
        P(),
    )
    out_specs = (P(None, ("dom", "ml")), P("dom", None, "ml"))
    return jax.shard_map(
        functools.partial(on_device, shape),
        mesh=mesh,
        in_specs=in_specs,
        out_specs=out_specs,
        check_vma=False,
    )
```

```python
import functools
import math

import jax
import jax.numpy as jnp
from jax import lax
from jax.experimental import pallas as pl
from jax.experimental.pallas import tpu as pltpu
from jax.sharding import PartitionSpec as P

TILE = 128
RADIUS = 6.0
SOFTEN = 1.0
COULOMB = 0.5
CHUNK = 64
WAVE = (0.261799388, -0.00299057413, 1.02484123e-05, -1.67106067e-08, 1.52995984e-11)
F32 = jnp.float32
BF16 = jnp.bfloat16
MESH = pl.DeviceIdType.MESH
ANY = pl.BlockSpec(memory_space=pl.ANY)
VMEM = pl.BlockSpec(memory_space=pltpu.VMEM)


def split3(x):
    high = x.astype(BF16).astype(F32)
    rest = x - high
    middle = rest.astype(BF16).astype(F32)
    return high, middle, (rest - middle).astype(BF16).astype(F32)


def last_row(shape):
    return lax.broadcasted_iota(jnp.int32, shape, 0) == 3


def left_factor(xyz):
    norm = jnp.sum(xyz * xyz, axis=0, keepdims=True)
    high, middle, low = split3(jnp.concatenate([xyz, norm], axis=0))
    last = last_row(high.shape)
    one = jnp.ones_like(high)
    groups = [
        high,
        jnp.where(last, middle, high),
        jnp.where(last, low, middle),
        jnp.where(last, one, high),
        jnp.where(last, one, low),
        jnp.where(last, one, middle),
        jnp.zeros_like(high),
        jnp.zeros_like(high),
    ]
    return jnp.concatenate(groups, axis=0)


def right_factor(xyz):
    norm = jnp.sum(xyz * xyz, axis=0, keepdims=True) + SOFTEN
    high, middle, low = split3(jnp.concatenate([-2.0 * xyz, norm], axis=0))
    last = last_row(high.shape)
    one = jnp.ones_like(high)
    groups = [
        jnp.where(last, one, high),
        jnp.where(last, one, middle),
        jnp.where(last, one, high),
        low,
        high,
        middle,
        jnp.zeros_like(high),
        jnp.zeros_like(high),
    ]
    return jnp.concatenate(groups, axis=0).astype(BF16)


def moment_rows(xyz, weight):
    rows = jnp.concatenate([xyz * weight, weight], axis=0)
    high, middle, low = split3(rows)
    return jnp.concatenate([high, middle, low, jnp.zeros_like(high)], axis=0).astype(BF16)


def folded(moments):
    return moments[0:4] + moments[4:8] + moments[8:12]


def dot(a, b):
    return jnp.dot(a, b, preferred_element_type=F32)


def half_wave(w):
    y = w * w
    p = WAVE[-1]
    for c in WAVE[-2::-1]:
        p = p * y + c
    return p * w


def kernel(
    shape,
    mm_pos,
    mm_charge,
    mm_tiles,
    feat,
    pos,
    nbr,
    msg_w,
    rad_w,
    out_w,
    read_w,
    mm_out,
    ml_out,
    win_p,
    win_q,
    tiles,
    feat_buf,
    nbr_own,
    pos_own,
    geo_own,
    geo_buf,
    msg_v,
    rad_v,
    out_v,
    read_v,
    turned,
    read_t,
    near_v,
    near_r,
    own_u,
    word_s,
    value_s,
    count_s,
    basis,
    spread,
    weight_s,
    rad_cols,
    stage,
    force_buf,
    local_sem,
    halo_send,
    halo_recv,
    ml_send,
    ml_recv,
    back_send,
    back_recv,
    all_in,
):
    doms, mls = shape
    patches = feat.shape[0]
    atoms = feat.shape[1]
    nbrs = nbr.shape[1]
    psize = mls * atoms
    layers, nb, width = rad_w.shape
    tile_nbrs, tile_count = mm_tiles.shape

    dom = lax.axis_index("dom")
    me = lax.axis_index("ml")
    flat = dom * mls + me
    after = lax.rem(flat + 1, doms * mls)
    before = lax.rem(flat + doms * mls - 1, doms * mls)
    sides = [(before // mls, lax.rem(before, mls)), (after // mls, lax.rem(after, mls))]
    my_patch = lax.rem(me, patches)

    loads = [
        pltpu.make_async_copy(nbr, nbr_own, local_sem.at[7]),
        pltpu.make_async_copy(pos, pos_own, local_sem.at[8]),
    ]
    local = [
        pltpu.make_async_copy(mm_pos, win_p.at[1], local_sem.at[0]),
        pltpu.make_async_copy(mm_charge, win_q.at[1], local_sem.at[1]),
        pltpu.make_async_copy(mm_tiles, tiles, local_sem.at[2]),
        pltpu.make_async_copy(msg_w, msg_v, local_sem.at[3]),
        pltpu.make_async_copy(rad_w, rad_v, local_sem.at[4]),
        pltpu.make_async_copy(out_w, out_v, local_sem.at[5]),
        pltpu.make_async_copy(read_w, read_v, local_sem.at[6]),
        pltpu.make_async_copy(feat.at[my_patch], feat_buf.at[me], local_sem.at[9]),
    ]
    for copy in loads + local:
        copy.start()

    barrier = pltpu.get_barrier_semaphore()
    low, high = me == 0, me == mls - 1
    edge = low | high
    for target in range(1, mls - 1):

        @pl.when(me != target)
        def _():
            pl.semaphore_signal(barrier, inc=1, device_id=(dom, target), device_id_type=MESH)

    for at_edge, side in zip((low, high), sides):

        @pl.when(at_edge)
        def _():
            pl.semaphore_signal(barrier, inc=1, device_id=side, device_id_type=MESH)

    peers = [lax.rem(me + o, mls) for o in range(1, mls)]

    for copy in loads:
        copy.wait()
    quarter = nbrs // 4
    assert nbrs % 4 == 0 and psize & (psize - 1) == 0 and psize <= 4096
    for p in range(patches):
        pairs = nbr_own[p, : 2 * quarter] + psize * nbr_own[p, 2 * quarter :]
        pairs = jnp.concatenate([pairs[:quarter], pairs[quarter:]], axis=1)
        geo_own[p, :quarter] = pairs.astype(F32)
        geo_own[p, quarter : quarter + 3, :atoms] = pos_own[:, p, :]
        geo_own[p, quarter : quarter + 3, atoms:] = pos_own[:, p, :]
        geo_own[p, quarter + 3 :] = jnp.zeros((geo_own.shape[1] - quarter - 3, 2 * atoms), F32)

    @pl.when(jnp.logical_not(edge))
    def _():
        pl.semaphore_wait(barrier, mls - 1)

    for inner, outer in ((1, 0), (mls - 2, mls - 1)):

        @pl.when(me == inner)
        def _():
            pl.semaphore_signal(all_in, inc=1, device_id=(dom, outer), device_id_type=MESH)

    @pl.when(edge)
    def _():
        pl.semaphore_wait(all_in, 1)


    halo = []
    for k, (side, slab) in enumerate(zip(sides, (2, 0))):
        for m, (src, dst) in enumerate(((mm_pos, win_p), (mm_charge, win_q))):
            halo.append(
                pltpu.make_async_remote_copy(
                    src_ref=src,
                    dst_ref=dst.at[slab],
                    send_sem=halo_send.at[2 * k + m],
                    recv_sem=halo_recv.at[2 * k + m],
                    device_id=side,
                    device_id_type=MESH,
                )
            )
    moves = []
    for m, (src, dst) in enumerate(((geo_own, geo_buf), (feat, feat_buf))):
        group = []
        for o, peer in enumerate(peers):
            group.append(
                pltpu.make_async_remote_copy(
                    src_ref=src.at[lax.rem(peer, patches)],
                    dst_ref=dst.at[me],
                    send_sem=ml_send.at[m, o],
                    recv_sem=ml_recv.at[m, o],
                    device_id=(dom, peer),
                    device_id_type=MESH,
                )
            )
        for copy in group:
            copy.start()
        moves.append(group)
    for k, at_edge in enumerate((low, high)):

        @pl.when(jnp.logical_not(at_edge))
        def _():
            for copy in halo[2 * k : 2 * k + 2]:
                copy.start()


    geo_buf[me] = geo_own[my_patch]
    for copy in local:
        copy.wait()
    for l in range(layers):
        turned[l] = msg_v[l].astype(F32).T.astype(BF16)
        turned[layers + l] = out_v[l].astype(F32).T.astype(BF16)
    read_t[...] = read_v[...].astype(F32).T.astype(BF16)
    center = nb // 2
    step = RADIUS / nb
    factors = [
        math.exp(-2.0 * (step * (n - center)) ** 2) / math.sqrt(nbrs) for n in range(nb)
    ]
    for l in range(layers):
        columns = jnp.concatenate([rad_v[l], jnp.zeros((width - nb, width), F32)], axis=0).T
        for n in range(nb):
            rad_cols[l, n] = jnp.broadcast_to(columns[:, n : n + 1] * factors[n], (width, TILE))
    left = left_factor(win_p[1])
    for t in range(tile_count):
        own_u[t] = left[:, t * TILE : (t + 1) * TILE].T.astype(BF16)

    def near_slab(slab):
        xyz = win_p[slab]
        right = right_factor(xyz)
        rows = moment_rows(xyz, win_q[slab])
        for t in range(tile_count):
            near_v[slab * tile_count + t] = right[:, t * TILE : (t + 1) * TILE]
            near_r[slab * tile_count + t] = rows[:, t * TILE : (t + 1) * TILE]

    near_slab(1)

    def mm_tile(t, carry):
        own = own_u[t]
        total = jnp.zeros((16, TILE), F32)
        for c in range(0, tile_nbrs, 2):
            one, two = tiles[c, t], tiles[c + 1, t]
            right = jnp.concatenate([near_v[one], near_v[two]], axis=1)
            rows = jnp.concatenate([near_r[one], near_r[two]], axis=1)
            inverse = lax.rsqrt(dot(own, right))
            cubed = (inverse * inverse * inverse).astype(BF16)
            total = total + lax.dot_general(
                rows, cubed, (((1,), (1,)), ((), ())), preferred_element_type=F32
            )
        at = pl.ds(pl.multiple_of(t * TILE, TILE), TILE)
        sums = folded(total)
        force = win_p[1, :, at] * sums[3:4] - sums[0:3]
        mm_out[:, at] = force * (COULOMB * win_q[1, :, at])
        return carry

    @pl.when(edge)
    def _():
        pl.semaphore_wait(barrier, 1)

    for k, at_edge in enumerate((low, high)):

        @pl.when(at_edge)
        def _():
            for copy in halo[2 * k : 2 * k + 2]:
                copy.start()

    for copy in moves[0]:
        copy.wait_recv()
    pieces = [geo_buf[d] for d in range(mls)]
    pairs = jnp.concatenate(
        [
            jnp.concatenate([piece[:quarter, :atoms] for piece in pieces], axis=1),
            jnp.concatenate([piece[:quarter, atoms:] for piece in pieces], axis=1),
        ],
        axis=0,
    ).astype(jnp.int32)
    bits = psize.bit_length() - 1
    listed = jnp.concatenate([pairs & (psize - 1), jnp.right_shift(pairs, bits)], axis=0)
    words = psize // 4
    half = psize // 8
    word_s[...] = listed & (half - 1)
    value_s[...] = jnp.left_shift(1, 4 * jnp.right_shift(listed, bits - 3))
    xyz = jnp.concatenate([piece[quarter : quarter + 3, :atoms] for piece in pieces], axis=1)
    senders = left_factor(xyz).T.astype(BF16)
    receivers = right_factor(xyz)
    rows = moment_rows(xyz, jnp.ones_like(xyz[0:1]))
    weight_s[...] = dot(senders, receivers)
    for ib in range(psize // TILE):
        at = slice(ib * TILE, (ib + 1) * TILE)
        place = lax.broadcasted_iota(jnp.int32, (words // 2, TILE), 0)
        even = jnp.zeros((words // 2, TILE), jnp.int32)
        odd = even
        for first in range(0, nbrs, 15):
            counts = jnp.zeros((words // 2, TILE), jnp.int32)
            for k in range(first, min(first + 15, nbrs)):
                hit = place == word_s[k : k + 1, at]
                counts = counts + jnp.where(hit, value_s[k : k + 1, at], 0)
            even = even + (counts & 0x0F0F0F0F)
            odd = odd + (jnp.right_shift(counts, 4) & 0x0F0F0F0F)
        count_s[: words // 2] = even
        count_s[words // 2 :] = odd
        for b in range(4):
            for c in range(0, words, CHUNK):
                row = b * words + c
                rows_at = slice(row, row + CHUNK)
                count = (jnp.right_shift(count_s[c : c + CHUNK], 8 * b) & 255).astype(F32)
                squared = weight_s[rows_at, at]
                distance = jnp.minimum(squared * lax.rsqrt(squared), RADIUS)
                wave = half_wave(RADIUS - distance)
                weight = count * (wave * wave)
                weight_s[rows_at, at] = weight
                shifted = distance - center * step
                scaled = shifted * (4.0 * step / math.log(2.0))
                middle = weight * jnp.exp2(shifted * shifted * (-2.0 / math.log(2.0)))
                up = jnp.exp2(scaled)
                down = jnp.exp2(-scaled)
                basis[center * psize + row : center * psize + row + CHUNK, at] = middle.astype(BF16)
                value = middle
                for n in range(center + 1, nb):
                    value = value * up
                    basis[n * psize + row : n * psize + row + CHUNK, at] = value.astype(BF16)
                value = middle
                for n in range(center - 1, -1, -1):
                    value = value * down
                    basis[n * psize + row : n * psize + row + CHUNK, at] = value.astype(BF16)

    for copy in moves[1]:
        copy.wait_recv()
    hidden = feat_buf[...].reshape(psize, width).astype(F32).T.astype(BF16)
    for l in range(layers):
        mixed = dot(turned[l], hidden).astype(BF16)
        wide = mixed.astype(F32)
        for n in range(nb):
            column = jnp.concatenate([rad_cols[l, n]] * (psize // TILE), axis=1)
            spread[:, n * psize : (n + 1) * psize] = (column * wide).astype(BF16)
        message = dot(spread[...], basis[...])
        active = (message / (1.0 + jnp.exp(-message))).astype(BF16)
        update = dot(turned[layers + l], active)
        hidden = (hidden.astype(F32) + update).astype(BF16)
    readout = dot(read_t[...], hidden)
    query = readout[:width].astype(BF16)
    key = readout[width:].T.astype(BF16)
    strength = dot(key, query) * weight_s[...] * (1.0 / width)
    strong = strength.astype(BF16)
    weak = (strength - strong.astype(F32)).astype(BF16)
    sums = folded(dot(rows, strong) + dot(rows, weak))
    force = sums[0:3] - xyz * sums[3:4]
    for d in range(mls):
        stage[d] = force[:, d * atoms : (d + 1) * atoms]
    group = me - my_patch
    returns = []
    for o in range(1, patches):
        owner = group + lax.rem(my_patch + o, patches)
        copy = pltpu.make_async_remote_copy(
            src_ref=stage.at[owner],
            dst_ref=force_buf.at[my_patch],
            send_sem=back_send.at[o - 1],
            recv_sem=back_recv.at[o - 1],
            device_id=(dom, owner),
            device_id_type=MESH,
        )
        copy.start()
        returns.append(copy)
    own = pltpu.make_async_copy(stage.at[me], force_buf.at[my_patch], local_sem.at[0])
    own.start()

    for copy in halo:
        copy.wait_recv()
    near_slab(0)
    near_slab(2)
    lax.fori_loop(0, tile_count, mm_tile, 0, unroll=True)

    for copy in halo:
        copy.wait_send()
    for group in moves:
        for copy in group:
            copy.wait_send()
    own.wait()
    for copy in returns:
        copy.wait()
    for p in range(patches):
        ml_out[:, p, :] = force_buf[p]


def on_device(
    shape,
    mm_positions,
    mm_charge,
    mm_tiles,
    ml_feat,
    ml_positions,
    ml_neighbours,
    msg_weight,
    radial_weight,
    out_weight,
    read_weight,
):
    mls = shape[1]
    patches, atoms, width = ml_feat.shape
    nbrs = ml_neighbours.shape[1]
    psize = mls * atoms
    layers, nb, _ = radial_weight.shape
    count = mm_positions.shape[1]
    tile_count = count // TILE
    dma = pltpu.SemaphoreType.DMA
    geo_rows = (nbrs // 4 + 3 + 7) // 8 * 8
    mm_force, ml_force = pl.pallas_call(
        functools.partial(kernel, shape),
        out_shape=(
            pltpu.VMEM((3, count), F32),
            pltpu.VMEM((3, patches, atoms), F32),
        ),
        in_specs=[ANY] * 10,
        out_specs=(VMEM, VMEM),
        scratch_shapes=[
            pltpu.VMEM((3, 3, count), F32),
            pltpu.VMEM((3, 1, count), F32),
            pltpu.SMEM(mm_tiles.shape[::-1], jnp.int32),
            pltpu.VMEM((mls, atoms, width), BF16),
            pltpu.VMEM((patches, nbrs, atoms), jnp.int32),
            pltpu.VMEM((3, patches, atoms), F32),
            pltpu.VMEM((patches, geo_rows, 2 * atoms), F32),
            pltpu.VMEM((mls, geo_rows, 2 * atoms), F32),
            pltpu.VMEM(msg_weight.shape, BF16),
            pltpu.VMEM(radial_weight.shape, F32),
            pltpu.VMEM(out_weight.shape, BF16),
            pltpu.VMEM(read_weight.shape, BF16),
            pltpu.VMEM((2 * layers, width, width), BF16),
            pltpu.VMEM(read_weight.shape[::-1], BF16),
            pltpu.VMEM((3 * tile_count, 32, TILE), BF16),
            pltpu.VMEM((3 * tile_count, 16, TILE), BF16),
            pltpu.VMEM((tile_count, TILE, 32), BF16),
            pltpu.VMEM((nbrs, psize), jnp.int32),
            pltpu.VMEM((nbrs, psize), jnp.int32),
            pltpu.VMEM((psize // 4, TILE), jnp.int32),
            pltpu.VMEM((nb * psize, psize), BF16),
            pltpu.VMEM((width, nb * psize), BF16),
            pltpu.VMEM((psize, psize), F32),
            pltpu.VMEM((layers, nb, width, TILE), F32),
            pltpu.VMEM((mls, 3, atoms), F32),
            pltpu.VMEM((patches, 3, atoms), F32),
            dma((10,)),
            dma((4,)),
            dma((4,)),
            dma((2, mls)),
            dma((2, mls)),
            dma((patches,)),
            dma((patches,)),
            pltpu.SemaphoreType.REGULAR,
        ],
        compiler_params=pltpu.CompilerParams(
            collective_id=0, has_side_effects=True, vmem_limit_bytes=60 * 1024 * 1024
        ),
        name="force_step",
    )(
        mm_positions,
        mm_charge.reshape(1, count),
        mm_tiles.T,
        ml_feat,
        ml_positions.transpose(1, 0, 2),
        ml_neighbours,
        msg_weight,
        radial_weight,
        out_weight,
        read_weight,
    )
    return mm_force, ml_force.transpose(1, 0, 2)


def solution(mesh):
    shape = (mesh.shape["dom"], mesh.shape["ml"])
    in_specs = (
        P(None, ("dom", "ml")),
        P(("dom", "ml")),
        P(("dom", "ml"), None),
        P("dom", "ml", None),
        P("dom", None, "ml"),
        P("dom", None, "ml"),
        P(),
        P(),
        P(),
        P(),
    )
    out_specs = (P(None, ("dom", "ml")), P("dom", None, "ml"))
    return jax.shard_map(
        functools.partial(on_device, shape),
        mesh=mesh,
        in_specs=in_specs,
        out_specs=out_specs,
        check_vma=False,
    )
```

```python
import functools
import math

import jax
import jax.numpy as jnp
from jax import lax
from jax.experimental import pallas as pl
from jax.experimental.pallas import tpu as pltpu
from jax.sharding import PartitionSpec as P

TILE = 128
RADIUS = 6.0
SOFTEN = 1.0
COULOMB = 0.5
CHUNK = 64
WAVE = (0.261799388, -0.00299057413, 1.02484123e-05, -1.67106067e-08, 1.52995984e-11)
F32 = jnp.float32
BF16 = jnp.bfloat16
MESH = pl.DeviceIdType.MESH
ANY = pl.BlockSpec(memory_space=pl.ANY)
VMEM = pl.BlockSpec(memory_space=pltpu.VMEM)


def split3(x):
    high = x.astype(BF16).astype(F32)
    rest = x - high
    middle = rest.astype(BF16).astype(F32)
    return high, middle, (rest - middle).astype(BF16).astype(F32)


def last_row(shape):
    return lax.broadcasted_iota(jnp.int32, shape, 0) == 3


def left_factor(xyz):
    norm = jnp.sum(xyz * xyz, axis=0, keepdims=True)
    high, middle, low = split3(jnp.concatenate([xyz, norm], axis=0))
    last = last_row(high.shape)
    one = jnp.ones_like(high)
    groups = [
        high,
        jnp.where(last, middle, high),
        jnp.where(last, low, middle),
        jnp.where(last, one, high),
        jnp.where(last, one, low),
        jnp.where(last, one, middle),
        jnp.zeros_like(high),
        jnp.zeros_like(high),
    ]
    return jnp.concatenate(groups, axis=0)


def right_factor(xyz):
    norm = jnp.sum(xyz * xyz, axis=0, keepdims=True) + SOFTEN
    high, middle, low = split3(jnp.concatenate([-2.0 * xyz, norm], axis=0))
    last = last_row(high.shape)
    one = jnp.ones_like(high)
    groups = [
        jnp.where(last, one, high),
        jnp.where(last, one, middle),
        jnp.where(last, one, high),
        low,
        high,
        middle,
        jnp.zeros_like(high),
        jnp.zeros_like(high),
    ]
    return jnp.concatenate(groups, axis=0).astype(BF16)


def moment_rows(xyz, weight):
    rows = jnp.concatenate([xyz * weight, weight], axis=0)
    high, middle, low = split3(rows)
    return jnp.concatenate([high, middle, low, jnp.zeros_like(high)], axis=0).astype(BF16)


def folded(moments):
    return moments[0:4] + moments[4:8] + moments[8:12]


def dot(a, b):
    return jnp.dot(a, b, preferred_element_type=F32)


def half_wave(w):
    y = w * w
    p = WAVE[-1]
    for c in WAVE[-2::-1]:
        p = p * y + c
    return p * w


def kernel(
    shape,
    mm_pos,
    mm_charge,
    mm_tiles,
    feat,
    pos,
    nbr,
    msg_w,
    rad_w,
    out_w,
    read_w,
    mm_out,
    ml_out,
    win_p,
    win_q,
    tiles,
    feat_buf,
    nbr_own,
    pos_own,
    geo_own,
    geo_buf,
    msg_v,
    rad_v,
    out_v,
    read_v,
    turned,
    read_t,
    near_v,
    near_r,
    own_u,
    word_s,
    value_s,
    count_s,
    basis,
    spread,
    weight_s,
    rad_cols,
    stage,
    force_buf,
    local_sem,
    halo_send,
    halo_recv,
    ml_send,
    ml_recv,
    back_send,
    back_recv,
    all_in,
):
    doms, mls = shape
    patches = feat.shape[0]
    atoms = feat.shape[1]
    nbrs = nbr.shape[1]
    psize = mls * atoms
    layers, nb, width = rad_w.shape
    tile_nbrs, tile_count = mm_tiles.shape

    dom = lax.axis_index("dom")
    me = lax.axis_index("ml")
    flat = dom * mls + me
    after = lax.rem(flat + 1, doms * mls)
    before = lax.rem(flat + doms * mls - 1, doms * mls)
    sides = [(before // mls, lax.rem(before, mls)), (after // mls, lax.rem(after, mls))]
    my_patch = lax.rem(me, patches)

    loads = [
        pltpu.make_async_copy(nbr, nbr_own, local_sem.at[7]),
        pltpu.make_async_copy(pos, pos_own, local_sem.at[8]),
    ]
    local = [
        pltpu.make_async_copy(mm_pos, win_p.at[1], local_sem.at[0]),
        pltpu.make_async_copy(mm_charge, win_q.at[1], local_sem.at[1]),
        pltpu.make_async_copy(mm_tiles, tiles, local_sem.at[2]),
        pltpu.make_async_copy(msg_w, msg_v, local_sem.at[3]),
        pltpu.make_async_copy(rad_w, rad_v, local_sem.at[4]),
        pltpu.make_async_copy(out_w, out_v, local_sem.at[5]),
        pltpu.make_async_copy(read_w, read_v, local_sem.at[6]),
        pltpu.make_async_copy(feat.at[my_patch], feat_buf.at[me], local_sem.at[9]),
    ]
    for copy in loads + local:
        copy.start()

    barrier = pltpu.get_barrier_semaphore()
    low, high = me == 0, me == mls - 1
    edge = low | high
    for target in range(1, mls - 1):

        @pl.when(me != target)
        def _():
            pl.semaphore_signal(barrier, inc=1, device_id=(dom, target), device_id_type=MESH)

    for at_edge, side in zip((low, high), sides):

        @pl.when(at_edge)
        def _():
            pl.semaphore_signal(barrier, inc=1, device_id=side, device_id_type=MESH)

    peers = [lax.rem(me + o, mls) for o in range(1, mls)]

    for copy in loads:
        copy.wait()
    quarter = nbrs // 4
    assert nbrs % 4 == 0 and psize & (psize - 1) == 0 and psize <= 4096
    for p in range(patches):
        pairs = nbr_own[p, : 2 * quarter] + psize * nbr_own[p, 2 * quarter :]
        pairs = jnp.concatenate([pairs[:quarter], pairs[quarter:]], axis=1)
        geo_own[p, :quarter] = pairs.astype(F32)
        geo_own[p, quarter : quarter + 3, :atoms] = pos_own[:, p, :]
        geo_own[p, quarter : quarter + 3, atoms:] = pos_own[:, p, :]
        geo_own[p, quarter + 3 :] = jnp.zeros((geo_own.shape[1] - quarter - 3, 2 * atoms), F32)

    @pl.when(jnp.logical_not(edge))
    def _():
        pl.semaphore_wait(barrier, mls - 1)

    for inner, outer in ((1, 0), (mls - 2, mls - 1)):

        @pl.when(me == inner)
        def _():
            pl.semaphore_signal(all_in, inc=1, device_id=(dom, outer), device_id_type=MESH)

    @pl.when(edge)
    def _():
        pl.semaphore_wait(all_in, 1)


    halo = []
    for k, (side, slab) in enumerate(zip(sides, (2, 0))):
        for m, (src, dst) in enumerate(((mm_pos, win_p), (mm_charge, win_q))):
            halo.append(
                pltpu.make_async_remote_copy(
                    src_ref=src,
                    dst_ref=dst.at[slab],
                    send_sem=halo_send.at[2 * k + m],
                    recv_sem=halo_recv.at[2 * k + m],
                    device_id=side,
                    device_id_type=MESH,
                )
            )
    moves = []
    for m, (src, dst) in enumerate(((geo_own, geo_buf), (feat, feat_buf))):
        group = []
        for o, peer in enumerate(peers):
            group.append(
                pltpu.make_async_remote_copy(
                    src_ref=src.at[lax.rem(peer, patches)],
                    dst_ref=dst.at[me],
                    send_sem=ml_send.at[m, o],
                    recv_sem=ml_recv.at[m, o],
                    device_id=(dom, peer),
                    device_id_type=MESH,
                )
            )
        for copy in group:
            copy.start()
        moves.append(group)
    for k, at_edge in enumerate((low, high)):

        @pl.when(jnp.logical_not(at_edge))
        def _():
            for copy in halo[2 * k : 2 * k + 2]:
                copy.start()


    geo_buf[me] = geo_own[my_patch]
    for copy in local:
        copy.wait()
    for l in range(layers):
        turned[l] = msg_v[l].astype(F32).T.astype(BF16)
        turned[layers + l] = out_v[l].astype(F32).T.astype(BF16)
    read_t[...] = read_v[...].astype(F32).T.astype(BF16)
    center = nb // 2
    step = RADIUS / nb
    factors = [
        math.exp(-2.0 * (step * (n - center)) ** 2) / math.sqrt(nbrs) for n in range(nb)
    ]
    for l in range(layers):
        columns = jnp.concatenate([rad_v[l], jnp.zeros((width - nb, width), F32)], axis=0).T
        for n in range(nb):
            rad_cols[l, n] = jnp.broadcast_to(columns[:, n : n + 1] * factors[n], (width, TILE))
    left = left_factor(win_p[1])
    for t in range(tile_count):
        own_u[t] = left[:, t * TILE : (t + 1) * TILE].T.astype(BF16)

    def near_slab(slab):
        xyz = win_p[slab]
        right = right_factor(xyz)
        rows = moment_rows(xyz, win_q[slab])
        for t in range(tile_count):
            near_v[slab * tile_count + t] = right[:, t * TILE : (t + 1) * TILE]
            near_r[slab * tile_count + t] = rows[:, t * TILE : (t + 1) * TILE]

    near_slab(1)

    def mm_tile(t, carry):
        own = own_u[t]
        cubes, rows = [], []
        for c in range(0, tile_nbrs, 2):
            one, two = tiles[c, t], tiles[c + 1, t]
            right = jnp.concatenate([near_v[one], near_v[two]], axis=1)
            rows += [near_r[one], near_r[two]]
            inverse = lax.rsqrt(dot(own, right))
            cubes.append((inverse * inverse * inverse).astype(BF16))
        total = lax.dot_general(
            jnp.concatenate(cubes, axis=1),
            jnp.concatenate(rows, axis=1),
            (((1,), (1,)), ((), ())),
            preferred_element_type=F32,
        ).T
        at = pl.ds(pl.multiple_of(t * TILE, TILE), TILE)
        sums = folded(total)
        force = win_p[1, :, at] * sums[3:4] - sums[0:3]
        mm_out[:, at] = force * (COULOMB * win_q[1, :, at])
        return carry

    @pl.when(edge)
    def _():
        pl.semaphore_wait(barrier, 1)

    for k, at_edge in enumerate((low, high)):

        @pl.when(at_edge)
        def _():
            for copy in halo[2 * k : 2 * k + 2]:
                copy.start()

    for copy in moves[0]:
        copy.wait_recv()
    pieces = [geo_buf[d] for d in range(mls)]
    pairs = jnp.concatenate(
        [
            jnp.concatenate([piece[:quarter, :atoms] for piece in pieces], axis=1),
            jnp.concatenate([piece[:quarter, atoms:] for piece in pieces], axis=1),
        ],
        axis=0,
    ).astype(jnp.int32)
    bits = psize.bit_length() - 1
    listed = jnp.concatenate([pairs & (psize - 1), jnp.right_shift(pairs, bits)], axis=0)
    words = psize // 4
    half = psize // 8
    word_s[...] = listed & (half - 1)
    value_s[...] = jnp.left_shift(1, 4 * jnp.right_shift(listed, bits - 3))
    xyz = jnp.concatenate([piece[quarter : quarter + 3, :atoms] for piece in pieces], axis=1)
    senders = left_factor(xyz).T.astype(BF16)
    receivers = right_factor(xyz)
    rows = moment_rows(xyz, jnp.ones_like(xyz[0:1]))
    weight_s[...] = dot(senders, receivers)
    for ib in range(psize // TILE):
        at = slice(ib * TILE, (ib + 1) * TILE)
        place = lax.broadcasted_iota(jnp.int32, (words // 2, TILE), 0)
        even = jnp.zeros((words // 2, TILE), jnp.int32)
        odd = even
        for first in range(0, nbrs, 15):
            counts = jnp.zeros((words // 2, TILE), jnp.int32)
            for k in range(first, min(first + 15, nbrs)):
                hit = place == word_s[k : k + 1, at]
                counts = counts + jnp.where(hit, value_s[k : k + 1, at], 0)
            even = even + (counts & 0x0F0F0F0F)
            odd = odd + (jnp.right_shift(counts, 4) & 0x0F0F0F0F)
        count_s[: words // 2] = even
        count_s[words // 2 :] = odd
        for b in range(4):
            for c in range(0, words, CHUNK):
                row = b * words + c
                rows_at = slice(row, row + CHUNK)
                count = (jnp.right_shift(count_s[c : c + CHUNK], 8 * b) & 255).astype(F32)
                squared = weight_s[rows_at, at]
                distance = jnp.minimum(squared * lax.rsqrt(squared), RADIUS)
                wave = half_wave(RADIUS - distance)
                weight = count * (wave * wave)
                weight_s[rows_at, at] = weight
                shifted = distance - center * step
                scaled = shifted * (4.0 * step / math.log(2.0))
                middle = weight * jnp.exp2(shifted * shifted * (-2.0 / math.log(2.0)))
                up = jnp.exp2(scaled)
                down = jnp.exp2(-scaled)
                basis[center * psize + row : center * psize + row + CHUNK, at] = middle.astype(BF16)
                value = middle
                for n in range(center + 1, nb):
                    value = value * up
                    basis[n * psize + row : n * psize + row + CHUNK, at] = value.astype(BF16)
                value = middle
                for n in range(center - 1, -1, -1):
                    value = value * down
                    basis[n * psize + row : n * psize + row + CHUNK, at] = value.astype(BF16)

    for copy in moves[1]:
        copy.wait_recv()
    hidden = feat_buf[...].reshape(psize, width).astype(F32).T.astype(BF16)
    for l in range(layers):
        mixed = dot(turned[l], hidden).astype(BF16)
        wide = mixed.astype(F32)
        for n in range(nb):
            column = jnp.concatenate([rad_cols[l, n]] * (psize // TILE), axis=1)
            spread[:, n * psize : (n + 1) * psize] = (column * wide).astype(BF16)
        message = dot(spread[...], basis[...])
        active = (message / (1.0 + jnp.exp(-message))).astype(BF16)
        update = dot(turned[layers + l], active)
        hidden = (hidden.astype(F32) + update).astype(BF16)
    readout = dot(read_t[...], hidden)
    query = readout[:width].astype(BF16)
    key = readout[width:].T.astype(BF16)
    strength = dot(key, query) * weight_s[...] * (1.0 / width)
    strong = strength.astype(BF16)
    weak = (strength - strong.astype(F32)).astype(BF16)
    sums = folded(dot(rows, strong) + dot(rows, weak))
    force = sums[0:3] - xyz * sums[3:4]
    for d in range(mls):
        stage[d] = force[:, d * atoms : (d + 1) * atoms]
    group = me - my_patch
    returns = []
    for o in range(1, patches):
        owner = group + lax.rem(my_patch + o, patches)
        copy = pltpu.make_async_remote_copy(
            src_ref=stage.at[owner],
            dst_ref=force_buf.at[my_patch],
            send_sem=back_send.at[o - 1],
            recv_sem=back_recv.at[o - 1],
            device_id=(dom, owner),
            device_id_type=MESH,
        )
        copy.start()
        returns.append(copy)
    own = pltpu.make_async_copy(stage.at[me], force_buf.at[my_patch], local_sem.at[0])
    own.start()

    for copy in halo:
        copy.wait_recv()
    near_slab(0)
    near_slab(2)
    lax.fori_loop(0, tile_count, mm_tile, 0, unroll=True)

    for copy in halo:
        copy.wait_send()
    for group in moves:
        for copy in group:
            copy.wait_send()
    own.wait()
    for copy in returns:
        copy.wait()
    for p in range(patches):
        ml_out[:, p, :] = force_buf[p]


def on_device(
    shape,
    mm_positions,
    mm_charge,
    mm_tiles,
    ml_feat,
    ml_positions,
    ml_neighbours,
    msg_weight,
    radial_weight,
    out_weight,
    read_weight,
):
    mls = shape[1]
    patches, atoms, width = ml_feat.shape
    nbrs = ml_neighbours.shape[1]
    psize = mls * atoms
    layers, nb, _ = radial_weight.shape
    count = mm_positions.shape[1]
    tile_count = count // TILE
    dma = pltpu.SemaphoreType.DMA
    geo_rows = (nbrs // 4 + 3 + 7) // 8 * 8
    mm_force, ml_force = pl.pallas_call(
        functools.partial(kernel, shape),
        out_shape=(
            pltpu.VMEM((3, count), F32),
            pltpu.VMEM((3, patches, atoms), F32),
        ),
        in_specs=[ANY] * 10,
        out_specs=(VMEM, VMEM),
        scratch_shapes=[
            pltpu.VMEM((3, 3, count), F32),
            pltpu.VMEM((3, 1, count), F32),
            pltpu.SMEM(mm_tiles.shape[::-1], jnp.int32),
            pltpu.VMEM((mls, atoms, width), BF16),
            pltpu.VMEM((patches, nbrs, atoms), jnp.int32),
            pltpu.VMEM((3, patches, atoms), F32),
            pltpu.VMEM((patches, geo_rows, 2 * atoms), F32),
            pltpu.VMEM((mls, geo_rows, 2 * atoms), F32),
            pltpu.VMEM(msg_weight.shape, BF16),
            pltpu.VMEM(radial_weight.shape, F32),
            pltpu.VMEM(out_weight.shape, BF16),
            pltpu.VMEM(read_weight.shape, BF16),
            pltpu.VMEM((2 * layers, width, width), BF16),
            pltpu.VMEM(read_weight.shape[::-1], BF16),
            pltpu.VMEM((3 * tile_count, 32, TILE), BF16),
            pltpu.VMEM((3 * tile_count, 16, TILE), BF16),
            pltpu.VMEM((tile_count, TILE, 32), BF16),
            pltpu.VMEM((nbrs, psize), jnp.int32),
            pltpu.VMEM((nbrs, psize), jnp.int32),
            pltpu.VMEM((psize // 4, TILE), jnp.int32),
            pltpu.VMEM((nb * psize, psize), BF16),
            pltpu.VMEM((width, nb * psize), BF16),
            pltpu.VMEM((psize, psize), F32),
            pltpu.VMEM((layers, nb, width, TILE), F32),
            pltpu.VMEM((mls, 3, atoms), F32),
            pltpu.VMEM((patches, 3, atoms), F32),
            dma((10,)),
            dma((4,)),
            dma((4,)),
            dma((2, mls)),
            dma((2, mls)),
            dma((patches,)),
            dma((patches,)),
            pltpu.SemaphoreType.REGULAR,
        ],
        compiler_params=pltpu.CompilerParams(
            collective_id=0, has_side_effects=True, vmem_limit_bytes=60 * 1024 * 1024
        ),
        name="force_step",
    )(
        mm_positions,
        mm_charge.reshape(1, count),
        mm_tiles.T,
        ml_feat,
        ml_positions.transpose(1, 0, 2),
        ml_neighbours,
        msg_weight,
        radial_weight,
        out_weight,
        read_weight,
    )
    return mm_force, ml_force.transpose(1, 0, 2)


def solution(mesh):
    shape = (mesh.shape["dom"], mesh.shape["ml"])
    in_specs = (
        P(None, ("dom", "ml")),
        P(("dom", "ml")),
        P(("dom", "ml"), None),
        P("dom", "ml", None),
        P("dom", None, "ml"),
        P("dom", None, "ml"),
        P(),
        P(),
        P(),
        P(),
    )
    out_specs = (P(None, ("dom", "ml")), P("dom", None, "ml"))
    return jax.shard_map(
        functools.partial(on_device, shape),
        mesh=mesh,
        in_specs=in_specs,
        out_specs=out_specs,
        check_vma=False,
    )
```
